128 devices in a mesh: row: 8 (over z_lo, x), col: 16 (over z_hi, y, core).
Axes of the slice: x: 4, y: 4, z: 4 (z_hi: 2, z_lo: 2; z = z_hi * 2 + z_lo), core: 2. Of those that a mesh axis runs over, the one named last changes fastest.
Arguments:
- amplitudes: float32 [2048, 8192], P('row', 'col'), may hold values from -6 to 6
- labels: int32 [16, 1], replicated, may hold values from 0 to 7, as said below
- integrals: float32 [8, 8192, 8192], P('row', None, 'col'), may hold values from -0.0625 to 0.0625
Outputs:
- residual: float32 [2048, 8192], P('row', 'col')
The draws below stay inside these ranges and needn't reach their ends.
Inputs may be any that keep to these rules, and one draw needn't show every extreme that they name: No irreducible representation labels more than 4 tiles, and one labels exactly 4.
All inputs are finite; a program needn't handle non-finite values.
Results may differ from the reference program's by a relative error of at most 0.00007.
Values sent between devices are 32-bit elements; how exact they have to be, the bound alone decides.
No kernel may reach another device: no remote copies, remote signals or barrier semaphores. Data moves between devices by JAX's collectives and lax.ppermute only.
A program may use at most 128 MiB of HBM per device.

```python
import jax
import jax.numpy as jnp
from jax import lax

IRREPS = 8
TILE = 128
WIDTH = 8192
RT = 2
NT = 16
AI = 2048
MOST = 4


def place_tile(order, slot, tile_id):
    found = jnp.argmax((order == tile_id).astype(jnp.int32)).astype(jnp.int32)
    current = order[slot]
    order = order.at[found].set(current)
    return order.at[slot].set(tile_id.astype(jnp.int32))


def draw_labels(key, part):
    key = jax.random.fold_in(key, 7)
    key_hot, key_order = jax.random.split(key)
    hot_irrep = jax.random.randint(key_hot, (), 0, IRREPS).astype(jnp.int32)
    position = jnp.arange(NT, dtype=jnp.int32)
    others = (hot_irrep + 1 + (position - MOST) % (IRREPS - 1)) % IRREPS
    listed = jnp.where(position < MOST, hot_irrep, others).astype(jnp.int32)
    row_count = NT // RT
    per_row = IRREPS // row_count
    owner_row = hot_irrep // per_row
    far_tile = ((owner_row + row_count // 2) % row_count * RT).astype(jnp.int32)
    near_tile = ((owner_row + row_count - 1) % row_count * RT).astype(jnp.int32)
    order = jax.random.permutation(key_order, NT).astype(jnp.int32)
    order = place_tile(order, 0, far_tile)
    order = place_tile(order, 1, near_tile)
    result = jnp.zeros((NT,), jnp.int32).at[order].set(listed)
    return result[:, None]


def shard_levels(rng, extent, cuts, smallest, high):
    level = 1.0
    for dim, shards_of in cuts:
        heights = jax.random.uniform(jax.random.fold_in(jax.random.fold_in(rng, 6), dim), (shards_of,), jnp.float32, smallest / len(cuts), high / len(cuts))
        level = level * jnp.repeat(jnp.exp(heights), extent[dim] // shards_of).reshape((-1,) + (1,) * (len(extent) - 1 - dim))
    return level


def gaussian(key, shape, scale, reach, pieces=(), kind=jnp.bfloat16):
    array = scale * jax.random.normal(key, shape, jnp.float32)
    if pieces:
        array = array * shard_levels(key, shape, pieces, -0.22, 0.18)
    return jnp.clip(array, -reach, reach).astype(kind)


def setup_inputs(seed: int = 0) -> dict:
    arg_keys = jax.random.split(jax.random.key(seed), 4)
    amplitudes = gaussian(arg_keys[0], (AI, WIDTH), 1.0, 6.0, ((0, 8), (1, 16)), jnp.float32)
    labels = draw_labels(jax.random.fold_in(arg_keys[3], 71), 0)
    integrals = gaussian(arg_keys[2], (IRREPS, WIDTH, WIDTH), WIDTH ** -0.5, 0.0625, ((0, 8), (2, 16)), jnp.float32)
    return {"amplitudes": amplitudes, "labels": labels, "integrals": integrals}


def reference(amplitudes, labels, integrals):
    row_blocks = amplitudes.reshape(-1, TILE, WIDTH)
    tile_irrep = labels[:, 0].astype(jnp.int32)

    def apply_tile(tile_pair):
        tile_rows, irrep_id = tile_pair
        weights = lax.dynamic_index_in_dim(integrals, irrep_id, 0, keepdims=False)
        return jnp.dot(tile_rows, weights, preferred_element_type=jnp.float32, precision=lax.Precision.HIGHEST)

    result_tiles = lax.map(apply_tile, (row_blocks, tile_irrep))
    return result_tiles.reshape(-1, WIDTH)
```

```python
import functools

import jax
import jax.numpy as jnp
import numpy as np
from jax import lax
from jax.experimental import pallas as pl
from jax.experimental.pallas import tpu as pltpu
from jax.sharding import PartitionSpec as P

TILE = 128
SLOTS = 4
CHUNKS = (64, 64)

ROWS = [(zl, x) for zl in range(2) for x in range(4)]
COLS = [(zh, y, c) for zh in range(2) for y in range(4) for c in range(2)]


def shift_x(a, dx):
    return lax.ppermute(a, "row", [(zl * 4 + x, zl * 4 + (x + dx) % 4) for zl, x in ROWS])


def flip_z(a):
    return lax.ppermute(a, "row", [(zl * 4 + x, (1 - zl) * 4 + x) for zl, x in ROWS])


def shift_y(a, dy):
    return lax.ppermute(
        a, "col", [(zh * 8 + y * 2 + c, zh * 8 + (y + dy) % 4 * 2 + c) for zh, y, c in COLS]
    )


def flip_core(a):
    return lax.ppermute(a, "col", [(i, i ^ 1) for i in range(16)])


def cross_z(a):
    pairs = [
        ((zl * 4 + x) * 16 + zh * 8 + i, ((1 - zl) * 4 + x) * 16 + (1 - zh) * 8 + i)
        for zl, x in ROWS
        for zh in range(2)
        for i in range(8)
    ]
    return lax.ppermute(a, ("row", "col"), pairs)


def split(v):
    hi = v.astype(jnp.bfloat16)
    return hi, (v - hi.astype(jnp.float32)).astype(jnp.bfloat16)


def product_kernel(n, first, at_ref, *refs):
    pieces, (own_ref, far_ref), refs = refs[:n], refs[n : n + 2], refs[n + 2 :]
    adds, (out_own, out_far) = refs[:2], refs[-2:]
    step = pl.program_id(0)

    for i, piece in enumerate(pieces):

        @pl.when(step == i)
        def _():
            a_hi, a_lo = split(piece[...])
            for j, (rhs, out) in enumerate(((own_ref, out_own), (far_ref, out_far))):
                b_hi, b_lo = split(rhs[...])
                dot = functools.partial(jnp.dot, preferred_element_type=jnp.float32)
                term = dot(a_hi, b_hi) + (dot(a_hi, b_lo) + dot(a_lo, b_hi))
                if i == 0:
                    out[...] = term if first else adds[j][...] + term
                else:
                    out[...] += term


def products(pieces, at, own, far, sums, after=()):
    n = len(pieces)
    m, width = pieces[0].shape
    cols = own.shape[1]
    whole = lambda shape: pl.BlockSpec(shape, lambda s, at: (0, 0))
    return pl.pallas_call(
        functools.partial(product_kernel, n, not sums),
        grid_spec=pltpu.PrefetchScalarGridSpec(
            num_scalar_prefetch=1,
            grid=(n,),
            in_specs=[whole((m, width))] * n
            + [
                pl.BlockSpec((width, cols), lambda s, at: (at[s], 0)),
                pl.BlockSpec((width, cols), lambda s, at: (at[s], 0)),
            ]
            + [whole((m, cols))] * len(sums)
            + [pl.BlockSpec(memory_space=pl.ANY)] * len(after),
            out_specs=[whole((m, cols))] * 2,
        ),
        out_shape=[jax.ShapeDtypeStruct((m, cols), jnp.float32)] * 2,
        compiler_params=pltpu.CompilerParams(vmem_limit_bytes=32 * 1024 * 1024),
        cost_estimate=pl.CostEstimate(
            flops=12 * n * m * width * cols,
            bytes_accessed=8 * n * width * cols + 4 * n * m * width,
            transcendentals=0,
        ),
        name="products",
    )(at, *pieces, own, far, *sums, *after)


def small_kernel(body, plan, shapes, operands, after=(), name=None):
    def kernel(plan_ref, *refs):
        body(plan_ref, refs[: len(operands)], refs[len(operands) + len(after) :])

    out = pl.pallas_call(
        kernel,
        in_specs=[pl.BlockSpec(memory_space=pltpu.SMEM)]
        + [pl.BlockSpec(memory_space=pltpu.VMEM)] * len(operands)
        + [pl.BlockSpec(memory_space=pl.ANY)] * len(after),
        out_specs=[pl.BlockSpec(memory_space=pltpu.VMEM)] * len(shapes),
        out_shape=[jax.ShapeDtypeStruct(s, jnp.float32) for s in shapes],
        compiler_params=pltpu.CompilerParams(vmem_limit_bytes=24 * 1024 * 1024),
        cost_estimate=pl.CostEstimate(
            flops=0, bytes_accessed=4 * sum(int(np.prod(s)) for s in shapes), transcendentals=0
        ),
        name=name,
    )(plan, *operands, *after)
    return out


def gather_rows(own):
    h = own.shape[1] // 2
    other = flip_z(own)
    below, above = shift_x(own, 1), shift_x(own, -1)
    below_o, above_o = shift_x(other, 1), shift_x(other, -1)
    far = [shift_x(below[:, :h], 1), shift_x(above[:, h:], -1)]
    far_o = [shift_x(below_o[:, :h], 1), shift_x(above_o[:, h:], -1)]
    return [[own], [other], [above], [above_o], far, far_o, [below], [below_o]]


def pick(plan, parts, after):
    m = parts[0][0].shape[1]
    width = parts[0][0].shape[2]
    flat_parts = [p for part in parts for p in part]

    def body(plan_ref, ins, outs):
        for s in range(2 * SLOTS):
            place = plan_ref[s]
            out, lo = outs[s // SLOTS], s % SLOTS * m
            k = 0
            for i, part in enumerate(parts):
                refs = ins[k : k + len(part)]
                k += len(part)

                @pl.when(place // 2 == i)
                def _():
                    at = lo
                    for ref in refs:
                        out[at : at + ref.shape[1]] = ref[place % 2]
                        at += ref.shape[1]

    return small_kernel(
        body, plan, [(SLOTS * m, width)] * 2, flat_parts, after, name="pick"
    )


def wait_for(values, *others):
    return lax.optimization_barrier((tuple(values), others))[0]


def cols_first(b, crossing):
    return shift_y(b, 1), shift_y(b, -1), cross_z(crossing)


def cols_second(below, above, bz):
    h = bz.shape[0] // 2
    far = shift_y(below[:h], 1), shift_y(above[h:], -1)
    return shift_y(bz, 1), shift_y(bz, -1), jnp.concatenate(far, axis=0)


def cols_third(below_z, above_z):
    h = below_z.shape[0] // 2
    return jnp.concatenate([shift_y(below_z[:h], 1), shift_y(above_z[h:], -1)], axis=0)


GROUPS = [[(0, 0), (0, 3), (0, 1), (1, 0)], [(0, 2), (1, 3), (1, 1)], [(1, 2)]]


def share(plan_ref, ex, product, lo, hi, out, at, arrived=None):
    for i in range(4):
        slot = plan_ref[2 * SLOTS + ex % 4 * 4 + i]

        @pl.when(slot >= 0)
        def _():
            out[i, at : at + hi - lo] = product[slot, lo:hi]

        @pl.when(slot < 0)
        def _():
            if arrived is None:
                out[i, at : at + hi - lo] = jnp.zeros((hi - lo, product.shape[2]), jnp.float32)
            else:
                out[i, at : at + hi - lo] = arrived(i)


def return_far(plan, sums):
    m, cols = sums[0].shape[0] // SLOTS, sums[0].shape[1]
    h = m // 2

    def body(plan_ref, ins, outs):
        mine, theirs = ins
        product, lower, upper = outs
        for s in range(SLOTS):
            rows = slice(s * m, (s + 1) * m)
            product[s] = mine[rows] + theirs[rows]
        share(plan_ref, 2, product, 0, h, lower, 0)
        share(plan_ref, 2, product, h, m, upper, 0)

    product, lower, upper = small_kernel(
        body,
        plan,
        [(SLOTS, m, cols), (4, h, cols), (4, h, cols)],
        [sums[0], flip_core(sums[1])],
        name="return_far",
    )
    return product, shift_x(lower, 1), shift_x(upper, -1)


def return_near(plan, product, from_below, from_above):
    _, m, cols = product.shape
    h = m // 2

    def body(plan_ref, ins, outs):
        product, from_below, from_above = ins
        up, down = outs
        share(plan_ref, 1, product, 0, h, up, 0, lambda i: from_below[i])
        share(plan_ref, 1, product, h, m, up, h)
        share(plan_ref, -1, product, 0, h, down, 0)
        share(plan_ref, -1, product, h, m, down, h, lambda i: from_above[i])

    up, down = small_kernel(
        body, plan, [(4, m, cols)] * 2, [product, from_below, from_above], name="return_near"
    )
    return product, shift_x(up, 1), shift_x(down, -1)


def return_here(plan, product, from_below, from_above):
    _, m, cols = product.shape

    def body(plan_ref, ins, outs):
        product, from_below, from_above = ins
        (total,) = outs
        share(plan_ref, 0, product, 0, m, total, 0, lambda i: from_below[i] + from_above[i])

    (total,) = small_kernel(
        body, plan, [(4, m, cols)], [product, from_below, from_above], name="return_here"
    )
    return total, flip_z(total[2:])


def on_device(amplitudes, labels, integrals):
    flat = labels[:, 0]
    n_tiles = flat.shape[0]
    local_tiles = amplitudes.shape[0] // TILE
    width = amplitudes.shape[1]
    cols = integrals.shape[2]
    row = lax.axis_index("row")
    col = lax.axis_index("col")
    zl, x = row // 4, row % 4
    zh, y, core = col // 8, col // 2 % 4, col % 2

    ids = np.arange(n_tiles, dtype=np.int32)
    same = (flat[:, None] == flat[None, :]) & (ids[None, :] < ids[:, None])
    rank = jnp.sum(same.astype(jnp.int32), axis=1)
    place = (ids // 2 % 4 - x) % 4 * 4 + ((ids // 8) ^ zl) * 2 + ids % 2
    slot = np.arange(2 * SLOTS, dtype=np.int32)
    target = jnp.where(slot < SLOTS, row, (1 - zl) * 4 + x)
    hit = (flat[None, :] == target[:, None]) & (rank[None, :] == (slot % SLOTS)[:, None])
    wanted = jnp.sum(jnp.where(hit, place[None, :], 0), axis=1)
    held = jnp.where(flat == row, rank, -1)
    slots = jnp.sum(jnp.where(place[None, :] == ids[:, None], held[None, :], 0), axis=1)
    plan = jnp.concatenate([wanted, slots])

    tiles = amplitudes.reshape(local_tiles, TILE, width)
    starts = [sum(CHUNKS[:i]) for i in range(len(CHUNKS))]
    pieces = [tiles[:, s : s + m] for s, m in zip(starts, CHUNKS)]
    parts = gather_rows(pieces[0])

    own = integrals.reshape(16 * width, cols)
    far = flip_core(own)
    at = []
    for group in GROUPS:
        gz, gy = np.array(group, np.int32).T
        places = (zh ^ gz) * 4 + (y + gy) % 4
        at.append(places * 2 + core)

    def step(group, blocks, sums, after=()):
        return products(blocks, at[group], own, far, sums, after)

    out, last = [], None
    for k in range(len(CHUNKS)):
        b, crossing = pick(plan, parts, () if last is None else last["seen"])
        if k + 1 < len(CHUNKS):
            ahead = wait_for([pieces[k + 1]], parts[3][0])
            parts = gather_rows(ahead[0])
        below, above, bz = cols_first(b, crossing)
        if last is not None:
            sums = step(1, last["second"], last["sums"], (b,))
            sums = step(2, last["third"], sums)
            below, above, bz = wait_for([below, above, bz], sums[0])
        below_z, above_z, far_b = cols_second(below, above, bz)
        ready = []
        if last is not None:
            back = return_far(plan, sums)
            ready = [back[0]]
        sums = step(0, [b, below, above, bz], [])
        far_z = cols_third(*wait_for([below_z, above_z], sums[0], *ready))
        if last is not None:
            out.append(return_here(plan, *return_near(plan, *back)))
        last = dict(
            seen=(below_z,), second=[far_b, below_z, above_z], third=[far_z], sums=sums
        )
    sums = step(1, last["second"], last["sums"], [t for t, _ in out[-1:]])
    sums = step(2, last["third"], sums)
    out.append(return_here(plan, *return_near(plan, *return_far(plan, sums))))
    out = [total[:2] + more for total, more in out]
    return jnp.concatenate(out, axis=1).reshape(local_tiles * TILE, cols)


def solution(mesh):
    in_specs = (P("row", "col"), P(), P("row", None, "col"))
    out_specs = P("row", "col")
    return jax.shard_map(
        on_device, mesh=mesh, in_specs=in_specs, out_specs=out_specs, check_vma=False
    )
```

```python
import functools

import jax
import jax.numpy as jnp
import numpy as np
from jax import lax
from jax.experimental import pallas as pl
from jax.experimental.pallas import tpu as pltpu
from jax.sharding import PartitionSpec as P

TILE = 128
SLOTS = 4
CHUNKS = (64, 64)

PLACES = [
    (zl, x, zh, y, c)
    for zl in range(2)
    for x in range(4)
    for zh in range(2)
    for y in range(4)
    for c in range(2)
]


def send(a, to):
    index = {p: i for i, p in enumerate(PLACES)}
    return lax.ppermute(a, ("row", "col"), [(i, index[to(*p)]) for p, i in index.items()])


def other_of(i, ring):
    return (i + (1 if i % 2 == ring else 3)) % 4


def swap_x(a, ring):
    return send(a, lambda zl, x, zh, y, c: (zl, other_of(x, ring), zh, y, c))


def swap_y(a, ring):
    return send(a, lambda zl, x, zh, y, c: (zl, x, zh, other_of(y, ring), c))


def flip_z(a):
    return send(a, lambda zl, x, zh, y, c: (1 - zl, x, zh, y, c))


def cross_z(a):
    return send(a, lambda zl, x, zh, y, c: (1 - zl, x, 1 - zh, y, c))


def flip_core(a):
    return send(a, lambda zl, x, zh, y, c: (zl, x, zh, y, 1 - c))


def split(v):
    hi = v.astype(jnp.bfloat16)
    return hi, (v - hi.astype(jnp.float32)).astype(jnp.bfloat16)


def product_kernel(blocks, n_arrays, first, at_ref, *refs):
    arrays, (own_ref, far_ref), refs = refs[:n_arrays], refs[n_arrays : n_arrays + 2], refs[n_arrays + 2 :]
    adds, (out_own, out_far) = refs[:2], refs[-2:]
    step = pl.program_id(0)

    for i, block in enumerate(blocks):

        @pl.when(step == i)
        def _():
            parts = [arrays[array][lo : lo + size] for array, lo, size in block]
            a_hi, a_lo = split(parts[0] if len(parts) == 1 else jnp.concatenate(parts, axis=0))
            for j, (rhs, out) in enumerate(((own_ref, out_own), (far_ref, out_far))):
                b_hi, b_lo = split(rhs[...])
                dot = functools.partial(jnp.dot, preferred_element_type=jnp.float32)
                term = dot(a_hi, b_hi) + (dot(a_hi, b_lo) + dot(a_lo, b_hi))
                if i == 0:
                    out[...] = term if first else adds[j][...] + term
                else:
                    out[...] += term


def products(arrays, blocks, at, own, far, sums):
    n = len(blocks)
    m = sum(size for _, _, size in blocks[0])
    width = arrays[0].shape[1]
    cols = own.shape[1]
    whole = lambda shape: pl.BlockSpec(shape, lambda s, at: (0, 0))
    return pl.pallas_call(
        functools.partial(product_kernel, blocks, len(arrays), not sums),
        grid_spec=pltpu.PrefetchScalarGridSpec(
            num_scalar_prefetch=1,
            grid=(n,),
            in_specs=[whole(a.shape) for a in arrays]
            + [pl.BlockSpec((width, cols), lambda s, at: (at[s], 0))] * 2
            + [whole((m, cols))] * len(sums),
            out_specs=[whole((m, cols))] * 2,
        ),
        out_shape=[jax.ShapeDtypeStruct((m, cols), jnp.float32)] * 2,
        compiler_params=pltpu.CompilerParams(vmem_limit_bytes=50 * 1024 * 1024),
        cost_estimate=pl.CostEstimate(
            flops=12 * n * m * width * cols,
            bytes_accessed=8 * n * width * cols + 4 * n * m * width,
            transcendentals=0,
        ),
        name="products",
    )(at, *arrays, own, far, *sums)


def small_kernel(body, plan, shapes, operands, after=(), name=None):
    def kernel(plan_ref, *refs):
        body(plan_ref, refs[: len(operands)], refs[len(operands) + len(after) :])

    out = pl.pallas_call(
        kernel,
        in_specs=[pl.BlockSpec(memory_space=pltpu.SMEM)]
        + [pl.BlockSpec(memory_space=pltpu.VMEM)] * len(operands)
        + [pl.BlockSpec(memory_space=pl.ANY)] * len(after),
        out_specs=[pl.BlockSpec(memory_space=pltpu.VMEM)] * len(shapes),
        out_shape=[jax.ShapeDtypeStruct(s, jnp.float32) for s in shapes],
        compiler_params=pltpu.CompilerParams(vmem_limit_bytes=24 * 1024 * 1024),
        cost_estimate=pl.CostEstimate(
            flops=0, bytes_accessed=4 * sum(int(np.prod(s)) for s in shapes), transcendentals=0
        ),
        name=name,
    )(plan, *operands, *after)
    return out


def wait_for(value, *others):
    return lax.optimization_barrier((value, others))[0]


def gather_second(near, other, swap, pieces=1):
    return swap(join(other, half(near[1], 0, pieces)), 0), swap(join(other, half(near[0], 1, pieces)), 1)


def gather_third(both, rows, swap, pieces=1):
    return swap(half(both[1][:rows], 0, pieces), 0), swap(half(both[0][:rows], 1, pieces), 1)


def join(*arrays):
    return jnp.concatenate(arrays, axis=0)


def half(a, which, pieces):
    cut = a.reshape(pieces, 2, -1, a.shape[1])[:, which]
    return cut.reshape(-1, a.shape[1])


def pick(plan, m, arrays, after):
    width = arrays[0].shape[1]
    h = m // 2
    where = [
        [(0, 0, m)],
        [(1, 0, m)],
        [(2, 0, m)],
        [(4, 0, m)],
        [(4, 2 * m, h), (5, 2 * m, h)],
        [(6, 0, h), (7, 0, h)],
        [(3, 0, m)],
        [(5, 0, m)],
    ]

    def body(plan_ref, ins, outs):
        for s in range(2 * SLOTS):
            place = plan_ref[s]
            out, to = outs[s // SLOTS], s % SLOTS * m
            for i, parts in enumerate(where):

                @pl.when(place // 2 == i)
                def _():
                    at = to
                    for array, lo, size in parts:
                        rows = pl.ds(pl.multiple_of(lo + place % 2 * size, 8), size)
                        out[at : at + size] = ins[array][rows]
                        at += size

    return small_kernel(body, plan, [(SLOTS * m, width)] * 2, arrays, after, name="pick")


GROUPS = [[(0, 0), (0, 1), (0, 3), (1, 0)], [(1, 1), (1, 3), (0, 2)], [(1, 2)]]


def share(plan_ref, ring, dz, product, lo, hi, out, at, pitch, arrived=None):
    for j in range(2):
        slot = plan_ref[2 * SLOTS + ring * 4 + dz * 2 + j]
        rows = pl.ds(at + j * pitch, hi - lo)

        @pl.when(slot >= 0)
        def _():
            out[rows] = product[slot, lo:hi]

        @pl.when(slot < 0)
        def _():
            if arrived is None:
                out[rows] = jnp.zeros((hi - lo, product.shape[2]), jnp.float32)
            else:
                out[rows] = arrived(j)


def return_first(plan, sums, swapped):
    m, cols = sums[0].shape[0] // SLOTS, sums[0].shape[1]
    h = m // 2

    def body(plan_ref, ins, outs):
        mine, theirs = ins
        product, out_a, out_b = outs
        for s in range(SLOTS):
            rows = slice(s * m, (s + 1) * m)
            product[s] = mine[rows] + theirs[rows]
        share(plan_ref, 2, 1, product, 0, h, out_a, 0, h)
        share(plan_ref, 2, 1, product, h, m, out_b, 0, h)

    shapes = [(SLOTS, m, cols), (m, cols), (m, cols)]
    product, a, b = small_kernel(body, plan, shapes, [sums[0], swapped], name="return_first")
    return product, [swap_x(a, 0), swap_x(b, 1)]


def near_shares(plan_ref, dz, product, out_a, out_b, from_a, from_b):
    m = product.shape[1]
    h = m // 2
    share(plan_ref, 1, dz, product, 0, h, out_a, 0, m)
    share(plan_ref, 1, dz, product, h, m, out_a, h, m, from_b)
    share(plan_ref, 3, dz, product, 0, h, out_b, 0, m, from_a)
    share(plan_ref, 3, dz, product, h, m, out_b, h, m)


def return_second(plan, product, came):
    _, m, cols = product.shape
    h = m // 2

    def body(plan_ref, ins, outs):
        product, a, b = ins
        out_a, out_b = outs
        part = lambda ref: lambda j: ref[j * h : (j + 1) * h]
        near_shares(plan_ref, 1, product, out_a, out_b, part(a), part(b))
        share(plan_ref, 2, 0, product, 0, h, out_a, 2 * m, h)
        share(plan_ref, 2, 0, product, h, m, out_b, 2 * m, h)

    a, b = small_kernel(
        body, plan, [(3 * m, cols)] * 2, [product, *came], name="return_second"
    )
    return [swap_x(a, 0), swap_x(b, 1)]


def return_third(plan, product, came):
    _, m, cols = product.shape
    h = m // 2

    def body(plan_ref, ins, outs):
        product, a, b = ins
        out_a, out_b, across = outs
        part = lambda ref: lambda j: ref[2 * m + j * h : 2 * m + (j + 1) * h]
        near_shares(plan_ref, 0, product, out_a, out_b, part(a), part(b))
        both = lambda j: a[j * m : (j + 1) * m] + b[j * m : (j + 1) * m]
        share(plan_ref, 0, 1, product, 0, m, across, 0, m, both)

    a, b, across = small_kernel(
        body, plan, [(2 * m, cols)] * 3, [product, *came], name="return_third"
    )
    return [swap_x(a, 0), swap_x(b, 1), flip_z(across)]


def return_last(plan, product, came):
    _, m, cols = product.shape

    def body(plan_ref, ins, outs):
        product, *came = ins
        (total,) = outs
        rows = lambda j: slice(j * m, (j + 1) * m)
        arrived = lambda j: came[0][rows(j)] + came[1][rows(j)] + came[2][rows(j)]
        share(plan_ref, 0, 0, product, 0, m, total, 0, m, arrived)

    (total,) = small_kernel(body, plan, [(2 * m, cols)], [product, *came], name="return_last")
    return total


def on_device(amplitudes, labels, integrals):
    flat = labels[:, 0]
    n_tiles = flat.shape[0]
    local_tiles = amplitudes.shape[0] // TILE
    width = amplitudes.shape[1]
    cols = integrals.shape[2]
    row = lax.axis_index("row")
    col = lax.axis_index("col")
    zl, x = row // 4, row % 4
    zh, y, core = col // 8, col // 2 % 4, col % 2

    ids = np.arange(n_tiles, dtype=np.int32)
    same = (flat[:, None] == flat[None, :]) & (ids[None, :] < ids[:, None])
    rank = jnp.sum(same.astype(jnp.int32), axis=1)
    ring = (ids // 2 % 4 - x) * (1 - 2 * (x % 2)) % 4
    place = ring * 4 + ((ids // 8) ^ zl) * 2 + ids % 2
    slot = np.arange(2 * SLOTS, dtype=np.int32)
    target = jnp.where(slot < SLOTS, row, (1 - zl) * 4 + x)
    hit = (flat[None, :] == target[:, None]) & (rank[None, :] == (slot % SLOTS)[:, None])
    wanted = jnp.sum(jnp.where(hit, place[None, :], 0), axis=1)
    held = jnp.where(flat == row, rank, -1)
    slots = jnp.sum(jnp.where(place[None, :] == ids[:, None], held[None, :], 0), axis=1)
    plan = jnp.concatenate([wanted, slots])

    tiles = amplitudes.reshape(local_tiles, TILE, width)
    starts = [sum(CHUNKS[:i]) for i in range(len(CHUNKS))]
    pieces = [tiles[:, s : s + m].reshape(-1, width) for s, m in zip(starts, CHUNKS)]

    own = integrals.reshape(16 * width, cols)
    far = flip_core(own)
    at = []
    for group in GROUPS:
        gz, ring = np.array(group, np.int32).T
        places = (zh ^ gz) * 4 + (y + ring * (1 - 2 * (y % 2))) % 4
        at.append(places * 2 + core)

    def rows_first(piece):
        return [piece, flip_z(piece), swap_x(piece, 0), swap_x(piece, 1)]

    def rows_second(arrays):
        return arrays + list(gather_second(arrays[2:4], arrays[1], swap_x, local_tiles))

    def rows_third(arrays):
        rows = arrays[1].shape[0]
        return arrays + list(gather_third(arrays[4:6], rows, swap_x, local_tiles))

    def step(group, last):
        m, h = last["m"], last["m"] // 2
        if group == 0:
            arrays, blocks = last["first"], [[(i, 0, m)] for i in range(4)]
        elif group == 1:
            arrays, blocks = last["second"], [[(0, 0, m)], [(1, 0, m)], [(0, m, h), (1, m, h)]]
        else:
            arrays, blocks = last["third"], [[(0, 0, h), (1, 0, h)]]
        last["sums"] = products(arrays, blocks, at[group], own, far, last["sums"])
        return last["sums"]

    arrays = rows_third(rows_second(rows_first(pieces[0])))
    out, last = [], None
    for k, m in enumerate(CHUNKS):
        more = k + 1 < len(CHUNKS)
        after = () if last is None else (last["second"][0], last["sums"][0])
        b, crossing = pick(plan, m, arrays, after)
        this = dict(m=SLOTS * m, sums=[])
        if more:
            arrays = rows_first(wait_for(pieces[k + 1], b))
        near = [swap_y(b, 0), swap_y(b, 1)]
        bz = cross_z(crossing)
        this["first"] = [b, *near, bz]
        ready = arrays if more else []
        if last is not None:
            step(1, last)
            sums = step(2, last)
            swapped = flip_core(sums[1])
            ready = [*ready, sums[0]]
        near, bz = wait_for((near, bz), *ready)
        this["second"] = gather_second(near, bz, swap_y)
        if more:
            arrays = rows_second(wait_for(arrays, near[0]))
        ready = arrays[4:6] if more else []
        if last is not None:
            product, came = return_first(plan, sums, swapped)
        step(0, this)
        if last is not None:
            came = return_second(plan, product, came)
            ready = [*ready, product]
        both = wait_for(this["second"], this["sums"][0], *ready)
        this["third"] = gather_third(both, SLOTS * m, swap_y)
        if more:
            arrays = rows_third(arrays)
        if last is not None:
            came = return_third(plan, product, came)
            out.append(return_last(plan, product, came))
        last = this
    last["sums"] = wait_for(last["sums"], *out)
    step(1, last)
    sums = step(2, last)
    product, came = return_first(plan, sums, flip_core(sums[1]))
    came = return_third(plan, product, return_second(plan, product, came))
    out.append(return_last(plan, product, came))
    out = [o.reshape(local_tiles, -1, cols) for o in out]
    return jnp.concatenate(out, axis=1).reshape(local_tiles * TILE, cols)


def solution(mesh):
    in_specs = (P("row", "col"), P(), P("row", None, "col"))
    out_specs = P("row", "col")
    return jax.shard_map(
        on_device, mesh=mesh, in_specs=in_specs, out_specs=out_specs, check_vma=False
    )
```

```python
import functools

import jax
import jax.numpy as jnp
import numpy as np
from jax import lax
from jax.experimental import pallas as pl
from jax.experimental.pallas import tpu as pltpu
from jax.sharding import PartitionSpec as P

TILE = 128
SLOTS = 4
CHUNKS = (64, 64)

PLACES = [
    (zl, x, zh, y, c)
    for zl in range(2)
    for x in range(4)
    for zh in range(2)
    for y in range(4)
    for c in range(2)
]


def send(a, to):
    index = {p: i for i, p in enumerate(PLACES)}
    return lax.ppermute(a, ("row", "col"), [(i, index[to(*p)]) for p, i in index.items()])


def other_of(i, ring):
    return (i + (1 if i % 2 == ring else 3)) % 4


def swap_x(a, ring):
    return send(a, lambda zl, x, zh, y, c: (zl, other_of(x, ring), zh, y, c))


def swap_y(a, ring):
    return send(a, lambda zl, x, zh, y, c: (zl, x, zh, other_of(y, ring), c))


def flip_z(a):
    return send(a, lambda zl, x, zh, y, c: (1 - zl, x, zh, y, c))


def cross_z(a):
    return send(a, lambda zl, x, zh, y, c: (1 - zl, x, 1 - zh, y, c))


def flip_core(a):
    return send(a, lambda zl, x, zh, y, c: (zl, x, zh, y, 1 - c))


def split(v):
    hi = v.astype(jnp.bfloat16)
    return hi, (v - hi.astype(jnp.float32)).astype(jnp.bfloat16)


def product_kernel(blocks, n_arrays, first, at_ref, *refs):
    arrays, (own_ref, far_ref), refs = refs[:n_arrays], refs[n_arrays : n_arrays + 2], refs[n_arrays + 2 :]
    adds, (out_own, out_far) = refs[:2], refs[-2:]
    step = pl.program_id(0)

    for i, block in enumerate(blocks):

        @pl.when(step == i)
        def _():
            parts = [arrays[array][lo : lo + size] for array, lo, size in block]
            a_hi, a_lo = split(parts[0] if len(parts) == 1 else jnp.concatenate(parts, axis=0))
            for j, (rhs, out) in enumerate(((own_ref, out_own), (far_ref, out_far))):
                b_hi, b_lo = split(rhs[...])
                dot = functools.partial(jnp.dot, preferred_element_type=jnp.float32)
                term = dot(a_hi, b_hi) + (dot(a_hi, b_lo) + dot(a_lo, b_hi))
                if i == 0:
                    out[...] = term if first else adds[j][...] + term
                else:
                    out[...] += term


def products(arrays, blocks, at, own, far, sums):
    n = len(blocks)
    m = sum(size for _, _, size in blocks[0])
    width = arrays[0].shape[1]
    cols = own.shape[1]
    whole = lambda shape: pl.BlockSpec(shape, lambda s, at: (0, 0))
    return pl.pallas_call(
        functools.partial(product_kernel, blocks, len(arrays), not sums),
        grid_spec=pltpu.PrefetchScalarGridSpec(
            num_scalar_prefetch=1,
            grid=(n,),
            in_specs=[whole(a.shape) for a in arrays]
            + [pl.BlockSpec((width, cols), lambda s, at: (at[s], 0))] * 2
            + [whole((m, cols))] * len(sums),
            out_specs=[whole((m, cols))] * 2,
        ),
        out_shape=[jax.ShapeDtypeStruct((m, cols), jnp.float32)] * 2,
        compiler_params=pltpu.CompilerParams(vmem_limit_bytes=50 * 1024 * 1024),
        cost_estimate=pl.CostEstimate(
            flops=12 * n * m * width * cols,
            bytes_accessed=8 * n * width * cols + 4 * n * m * width,
            transcendentals=0,
        ),
        name="products",
    )(at, *arrays, own, far, *sums)


def small_kernel(body, plan, shapes, operands, after=(), name=None):
    def kernel(plan_ref, *refs):
        body(plan_ref, refs[: len(operands)], refs[len(operands) + len(after) :])

    out = pl.pallas_call(
        kernel,
        in_specs=[pl.BlockSpec(memory_space=pltpu.SMEM)]
        + [pl.BlockSpec(memory_space=pltpu.VMEM)] * len(operands)
        + [pl.BlockSpec(memory_space=pl.ANY)] * len(after),
        out_specs=[pl.BlockSpec(memory_space=pltpu.VMEM)] * len(shapes),
        out_shape=[jax.ShapeDtypeStruct(s, jnp.float32) for s in shapes],
        compiler_params=pltpu.CompilerParams(vmem_limit_bytes=24 * 1024 * 1024),
        cost_estimate=pl.CostEstimate(
            flops=0, bytes_accessed=4 * sum(int(np.prod(s)) for s in shapes), transcendentals=0
        ),
        name=name,
    )(plan, *operands, *after)
    return out


def wait_for(value, *others):
    return lax.optimization_barrier((value, others))[0]


def gather_second(near, other, swap, pieces=1):
    return swap(join(other, half(near[1], 0, pieces)), 0), swap(join(other, half(near[0], 1, pieces)), 1)


def gather_third(both, rows, swap, pieces=1):
    return swap(half(both[1][:rows], 0, pieces), 0), swap(half(both[0][:rows], 1, pieces), 1)


def join(*arrays):
    return jnp.concatenate(arrays, axis=0)


def half(a, which, pieces):
    cut = a.reshape(pieces, 2, -1, a.shape[1])[:, which]
    return cut.reshape(-1, a.shape[1])


def pick(plan, m, arrays, after):
    width = arrays[0].shape[1]
    h = m // 2
    where = [
        [(0, 0, m)],
        [(1, 0, m)],
        [(2, 0, m)],
        [(4, 0, m)],
        [(4, 2 * m, h), (5, 2 * m, h)],
        [(6, 0, h), (7, 0, h)],
        [(3, 0, m)],
        [(5, 0, m)],
    ]

    def body(plan_ref, ins, outs):
        for s in range(2 * SLOTS):
            place = plan_ref[s]
            out, to = outs[s // SLOTS], s % SLOTS * m
            for i, parts in enumerate(where):

                @pl.when(place // 2 == i)
                def _():
                    at = to
                    for array, lo, size in parts:
                        rows = pl.ds(pl.multiple_of(lo + place % 2 * size, 8), size)
                        out[at : at + size] = ins[array][rows]
                        at += size

    return small_kernel(body, plan, [(SLOTS * m, width)] * 2, arrays, after, name="pick")


GROUPS = [[(0, 0), (0, 1), (0, 3), (1, 0)], [(1, 1), (1, 3), (0, 2)], [(1, 2)]]


def share(plan_ref, ring, dz, product, lo, hi, out, at, pitch, arrived=None):
    for j in range(2):
        slot = plan_ref[2 * SLOTS + ring * 4 + dz * 2 + j]
        rows = pl.ds(at + j * pitch, hi - lo)

        @pl.when(slot >= 0)
        def _():
            out[rows] = product[slot, lo:hi]

        @pl.when(slot < 0)
        def _():
            if arrived is None:
                out[rows] = jnp.zeros((hi - lo, product.shape[2]), jnp.float32)
            else:
                out[rows] = arrived(j)


def return_first(plan, sums, swapped):
    m, cols = sums[0].shape[0] // SLOTS, sums[0].shape[1]
    h = m // 2

    def body(plan_ref, ins, outs):
        mine, theirs = ins
        product, out_a, out_b = outs
        for s in range(SLOTS):
            rows = slice(s * m, (s + 1) * m)
            product[s] = mine[rows] + theirs[rows]
        share(plan_ref, 2, 1, product, 0, h, out_a, 0, h)
        share(plan_ref, 2, 1, product, h, m, out_b, 0, h)

    shapes = [(SLOTS, m, cols), (m, cols), (m, cols)]
    product, a, b = small_kernel(body, plan, shapes, [sums[0], swapped], name="return_first")
    return product, [swap_x(a, 0), swap_x(b, 1)]


def near_shares(plan_ref, dz, product, out_a, out_b, from_a, from_b):
    m = product.shape[1]
    h = m // 2
    share(plan_ref, 1, dz, product, 0, h, out_a, 0, m)
    share(plan_ref, 1, dz, product, h, m, out_a, h, m, from_b)
    share(plan_ref, 3, dz, product, 0, h, out_b, 0, m, from_a)
    share(plan_ref, 3, dz, product, h, m, out_b, h, m)


def return_second(plan, product, came):
    _, m, cols = product.shape
    h = m // 2

    def body(plan_ref, ins, outs):
        product, a, b = ins
        out_a, out_b = outs
        part = lambda ref: lambda j: ref[j * h : (j + 1) * h]
        near_shares(plan_ref, 1, product, out_a, out_b, part(a), part(b))
        share(plan_ref, 2, 0, product, 0, h, out_a, 2 * m, h)
        share(plan_ref, 2, 0, product, h, m, out_b, 2 * m, h)

    a, b = small_kernel(
        body, plan, [(3 * m, cols)] * 2, [product, *came], name="return_second"
    )
    return a, [swap_x(a, 0), swap_x(b, 1)]


def return_third(plan, product, came):
    _, m, cols = product.shape
    h = m // 2

    def body(plan_ref, ins, outs):
        product, a, b = ins
        out_a, out_b, across = outs
        part = lambda ref: lambda j: ref[2 * m + j * h : 2 * m + (j + 1) * h]
        near_shares(plan_ref, 0, product, out_a, out_b, part(a), part(b))
        both = lambda j: a[j * m : (j + 1) * m] + b[j * m : (j + 1) * m]
        share(plan_ref, 0, 1, product, 0, m, across, 0, m, both)

    a, b, across = small_kernel(
        body, plan, [(2 * m, cols)] * 3, [product, *came], name="return_third"
    )
    return [swap_x(a, 0), swap_x(b, 1), flip_z(across)]


def return_last(plan, product, came):
    _, m, cols = product.shape

    def body(plan_ref, ins, outs):
        product, *came = ins
        (total,) = outs
        rows = lambda j: slice(j * m, (j + 1) * m)
        arrived = lambda j: came[0][rows(j)] + came[1][rows(j)] + came[2][rows(j)]
        share(plan_ref, 0, 0, product, 0, m, total, 0, m, arrived)

    (total,) = small_kernel(body, plan, [(2 * m, cols)], [product, *came], name="return_last")
    return total


def on_device(amplitudes, labels, integrals):
    flat = labels[:, 0]
    n_tiles = flat.shape[0]
    local_tiles = amplitudes.shape[0] // TILE
    width = amplitudes.shape[1]
    cols = integrals.shape[2]
    row = lax.axis_index("row")
    col = lax.axis_index("col")
    zl, x = row // 4, row % 4
    zh, y, core = col // 8, col // 2 % 4, col % 2

    ids = np.arange(n_tiles, dtype=np.int32)
    same = (flat[:, None] == flat[None, :]) & (ids[None, :] < ids[:, None])
    rank = jnp.sum(same.astype(jnp.int32), axis=1)
    ring = (ids // 2 % 4 - x) * (1 - 2 * (x % 2)) % 4
    place = ring * 4 + ((ids // 8) ^ zl) * 2 + ids % 2
    slot = np.arange(2 * SLOTS, dtype=np.int32)
    target = jnp.where(slot < SLOTS, row, (1 - zl) * 4 + x)
    hit = (flat[None, :] == target[:, None]) & (rank[None, :] == (slot % SLOTS)[:, None])
    wanted = jnp.sum(jnp.where(hit, place[None, :], 0), axis=1)
    held = jnp.where(flat == row, rank, -1)
    slots = jnp.sum(jnp.where(place[None, :] == ids[:, None], held[None, :], 0), axis=1)
    plan = jnp.concatenate([wanted, slots])

    tiles = amplitudes.reshape(local_tiles, TILE, width)
    starts = [sum(CHUNKS[:i]) for i in range(len(CHUNKS))]
    pieces = [tiles[:, s : s + m].reshape(-1, width) for s, m in zip(starts, CHUNKS)]

    own = integrals.reshape(16 * width, cols)
    far = flip_core(own)
    at = []
    for group in GROUPS:
        gz, ring = np.array(group, np.int32).T
        places = (zh ^ gz) * 4 + (y + ring * (1 - 2 * (y % 2))) % 4
        at.append(places * 2 + core)

    def rows_first(piece):
        return [piece, flip_z(piece), swap_x(piece, 0), swap_x(piece, 1)]

    def rows_second(arrays):
        return arrays + list(gather_second(arrays[2:4], arrays[1], swap_x, local_tiles))

    def rows_third(arrays):
        rows = arrays[1].shape[0]
        return arrays + list(gather_third(arrays[4:6], rows, swap_x, local_tiles))

    def step(group, last):
        m, h = last["m"], last["m"] // 2
        if group == 0:
            arrays, blocks = last["first"], [[(i, 0, m)] for i in range(4)]
        elif group == 1:
            arrays, blocks = last["second"], [[(0, 0, m)], [(1, 0, m)], [(0, m, h), (1, m, h)]]
        else:
            arrays, blocks = last["third"], [[(0, 0, h), (1, 0, h)]]
        last["sums"] = products(arrays, blocks, at[group], own, far, last["sums"])
        return last["sums"]

    def finish(last, back):
        sums = step(1, last)
        if back is not None:
            product, came = back
            back = product, return_third(plan, product, wait_for(came, sums[0]))
        return step(2, last), back

    arrays = rows_third(rows_second(rows_first(pieces[0])))
    out, last, back = [], None, None
    for k, m in enumerate(CHUNKS):
        more = k + 1 < len(CHUNKS)
        after = () if last is None else (last["second"][0], last["sums"][0])
        b, crossing = pick(plan, m, arrays, after)
        this = dict(m=SLOTS * m, sums=[])
        if more:
            arrays = rows_first(wait_for(pieces[k + 1], b))
        near = [swap_y(b, 0), swap_y(b, 1)]
        bz = cross_z(crossing)
        this["first"] = [b, *near, bz]
        ready = arrays if more else []
        if last is not None:
            sums, back = finish(last, back)
            swapped = flip_core(sums[1])
            ready = [*ready, sums[0]]
        near, bz = wait_for((near, bz), *ready)
        this["second"] = gather_second(near, bz, swap_y)
        if more:
            arrays = rows_second(wait_for(arrays, near[0]))
        ready = arrays[4:6] if more else []
        if last is not None:
            product, came = return_first(plan, sums, swapped)
        step(0, this)
        if last is not None:
            if back is not None:
                out.append(return_last(plan, *back))
            sent, came = return_second(plan, product, wait_for(came, this["sums"][0], *out))
            back = product, came
            ready = [*ready, sent]
        both = wait_for(this["second"], this["sums"][0], *ready)
        this["third"] = gather_third(both, SLOTS * m, swap_y)
        if more:
            arrays = rows_third(wait_for(arrays, this["sums"][0]))
        last = this
    sums, back = finish(last, back)
    product, came = return_first(plan, sums, flip_core(sums[1]))
    if back is not None:
        out.append(return_last(plan, *back))
    came = return_second(plan, product, wait_for(came, *out))[1]
    out.append(return_last(plan, product, return_third(plan, product, came)))
    out = [o.reshape(local_tiles, -1, cols) for o in out]
    return jnp.concatenate(out, axis=1).reshape(local_tiles * TILE, cols)


def solution(mesh):
    in_specs = (P("row", "col"), P(), P("row", None, "col"))
    out_specs = P("row", "col")
    return jax.shard_map(
        on_device, mesh=mesh, in_specs=in_specs, out_specs=out_specs, check_vma=False
    )
```

```python
import functools

import jax
import jax.numpy as jnp
import numpy as np
from jax import lax
from jax.experimental import pallas as pl
from jax.experimental.pallas import tpu as pltpu
from jax.sharding import PartitionSpec as P

TILE = 128
SLOTS = 4
CHUNKS = (64, 64)
BRIEF = pl.CostEstimate(flops=1, bytes_accessed=1, transcendentals=0)

PLACES = [
    (zl, x, zh, y, c)
    for zl in range(2)
    for x in range(4)
    for zh in range(2)
    for y in range(4)
    for c in range(2)
]


def send(a, to):
    index = {p: i for i, p in enumerate(PLACES)}
    return lax.ppermute(a, ("row", "col"), [(i, index[to(*p)]) for p, i in index.items()])


def other_of(i, ring):
    return (i + (1 if i % 2 == ring else 3)) % 4


def swap_x(a, ring):
    return send(a, lambda zl, x, zh, y, c: (zl, other_of(x, ring), zh, y, c))


def swap_y(a, ring):
    return send(a, lambda zl, x, zh, y, c: (zl, x, zh, other_of(y, ring), c))


def flip_z(a):
    return send(a, lambda zl, x, zh, y, c: (1 - zl, x, zh, y, c))


def cross_z(a):
    return send(a, lambda zl, x, zh, y, c: (1 - zl, x, 1 - zh, y, c))


def flip_core(a):
    return send(a, lambda zl, x, zh, y, c: (zl, x, zh, y, 1 - c))


def split(v):
    hi = v.astype(jnp.bfloat16)
    return hi, (v - hi.astype(jnp.float32)).astype(jnp.bfloat16)


def split_rows(a, width, at, first, parts=None):
    n, cols = at.shape[0], a.shape[1]

    def kernel(at_ref, a_ref, *refs):
        def body(a, hi, lo):
            hi[...], lo[...] = split(a[...])

        pltpu.emit_pipeline(
            body,
            grid=(n,),
            in_specs=[pl.BlockSpec((width, cols), lambda s: (at_ref[s], 0))],
            out_specs=[pl.BlockSpec((width, cols), lambda s: (s, 0))] * 2,
        )(a_ref, refs[-1].at[first], refs[-1].at[first + 1])

    before = () if parts is None else (parts,)
    anywhere = pl.BlockSpec(memory_space=pl.ANY)
    return pl.pallas_call(
        kernel,
        in_specs=[pl.BlockSpec(memory_space=pltpu.SMEM), anywhere] + [anywhere] * len(before),
        out_specs=anywhere,
        out_shape=jax.ShapeDtypeStruct((4, n * width, cols), jnp.bfloat16),
        input_output_aliases={2: 0} if before else {},
        compiler_params=pltpu.CompilerParams(vmem_limit_bytes=50 * 1024 * 1024),
        cost_estimate=BRIEF,
        name="split_rows",
    )(at, a, *before)


def products(arrays, blocks, at, rhs, sums):
    n = len(blocks)
    m = sum(size for _, _, size in blocks[0])
    width = arrays[0].shape[1]
    cols = rhs.shape[2]
    dot = functools.partial(jnp.dot, preferred_element_type=jnp.float32)

    def kernel(at_ref, *refs):
        ins, refs = refs[: len(arrays)], refs[len(arrays) :]
        rhs_ref, *refs = refs
        adds, (*outs, held, sems) = refs[: len(sums)], refs[len(sums) :]

        def copies(i):
            rows = pl.ds(pl.multiple_of(at_ref[i] * width, width), width)
            return [
                pltpu.make_async_copy(rhs_ref.at[j, rows], held.at[i, j], sems.at[i, j])
                for j in range(4)
            ]

        for i in range(n):
            for copy in copies(i):
                copy.start()
        for i, block in enumerate(blocks):
            rows = [ins[array][lo : lo + size] for array, lo, size in block]
            a_hi, a_lo = split(rows[0] if len(rows) == 1 else jnp.concatenate(rows, axis=0))
            a_both = jnp.concatenate([a_hi, a_lo], axis=0)
            for copy in copies(i):
                copy.wait()
            for j, out in enumerate(outs):
                upper = dot(a_both, held[i, 2 * j])
                term = upper[:m] + (upper[m:] + dot(a_hi, held[i, 2 * j + 1]))
                if i == 0:
                    out[...] = adds[j][...] + term if sums else term
                else:
                    out[...] += term

    vmem = pl.BlockSpec(memory_space=pltpu.VMEM)
    return pl.pallas_call(
        kernel,
        in_specs=[pl.BlockSpec(memory_space=pltpu.SMEM)]
        + [vmem] * len(arrays)
        + [pl.BlockSpec(memory_space=pl.ANY)]
        + [vmem] * len(sums),
        out_specs=[vmem] * 2,
        out_shape=[jax.ShapeDtypeStruct((m, cols), jnp.float32)] * 2,
        scratch_shapes=[
            pltpu.VMEM((n, 4, width, cols), jnp.bfloat16),
            pltpu.SemaphoreType.DMA((n, 4)),
        ],
        compiler_params=pltpu.CompilerParams(vmem_limit_bytes=50 * 1024 * 1024),
        cost_estimate=BRIEF,
        name="products",
    )(at, *arrays, rhs, *sums)


def small_kernel(body, plan, shapes, operands, after=(), name=None):
    def kernel(plan_ref, *refs):
        body(plan_ref, refs[: len(operands)], refs[len(operands) + len(after) :])

    out = pl.pallas_call(
        kernel,
        in_specs=[pl.BlockSpec(memory_space=pltpu.SMEM)]
        + [pl.BlockSpec(memory_space=pltpu.VMEM)] * len(operands)
        + [pl.BlockSpec(memory_space=pl.ANY)] * len(after),
        out_specs=[pl.BlockSpec(memory_space=pltpu.VMEM)] * len(shapes),
        out_shape=[jax.ShapeDtypeStruct(s, jnp.float32) for s in shapes],
        compiler_params=pltpu.CompilerParams(vmem_limit_bytes=24 * 1024 * 1024),
        cost_estimate=BRIEF,
        name=name,
    )(plan, *operands, *after)
    return out


def wait_for(value, *others):
    return lax.optimization_barrier((value, others))[0]


def gather_second(near, other, swap, pieces=1):
    going = [join(other, half(near[1 - i], i, pieces)) for i in range(2)]
    return going, [swap(a, i) for i, a in enumerate(going)]


def gather_third(both, rows, swap, pieces=1):
    going = [half(both[1 - i][:rows], i, pieces) for i in range(2)]
    return going, [swap(a, i) for i, a in enumerate(going)]


def join(*arrays):
    return jnp.concatenate(arrays, axis=0)


def half(a, which, pieces):
    cut = a.reshape(pieces, 2, -1, a.shape[1])[:, which]
    return cut.reshape(-1, a.shape[1])


def pick(plan, start, m, arrays, after):
    width = arrays[0].shape[1]
    h = m // 2
    where = [
        [(0, start, TILE, m)],
        [(1, start, TILE, m)],
        [(2, start, TILE, m)],
        [(4, 0, m, m)],
        [(4, 2 * m, h, h), (5, 2 * m, h, h)],
        [(6, 0, h, h), (7, 0, h, h)],
        [(3, start, TILE, m)],
        [(5, 0, m, m)],
    ]

    def body(plan_ref, ins, outs):
        for s in range(2 * SLOTS):
            place = plan_ref[s]
            out, to = outs[s // SLOTS], s % SLOTS * m
            for i, parts in enumerate(where):

                @pl.when(place // 2 == i)
                def _():
                    at = to
                    for array, lo, pitch, size in parts:
                        rows = pl.ds(pl.multiple_of(lo + place % 2 * pitch, 8), size)
                        out[at : at + size] = ins[array][rows]
                        at += size

    return small_kernel(body, plan, [(SLOTS * m, width)] * 2, arrays, after, name="pick")


GROUPS = [[(0, 0), (0, 1), (0, 3), (1, 0)], [(1, 1), (1, 3), (0, 2)], [(1, 2)]]


def share(plan_ref, ring, dz, product, lo, hi, out, at, pitch, arrived=None):
    for j in range(2):
        slot = plan_ref[2 * SLOTS + ring * 4 + dz * 2 + j]
        rows = pl.ds(at + j * pitch, hi - lo)

        @pl.when(slot >= 0)
        def _():
            out[rows] = product[slot, lo:hi]

        @pl.when(slot < 0)
        def _():
            if arrived is None:
                out[rows] = jnp.zeros((hi - lo, product.shape[2]), jnp.float32)
            else:
                out[rows] = arrived(j)


def return_first(plan, sums, swapped):
    m, cols = sums[0].shape[0] // SLOTS, sums[0].shape[1]
    h = m // 2

    def body(plan_ref, ins, outs):
        mine, theirs = ins
        product, out_a, out_b = outs
        for s in range(SLOTS):
            rows = slice(s * m, (s + 1) * m)
            product[s] = mine[rows] + theirs[rows]
        share(plan_ref, 2, 1, product, 0, h, out_a, 0, h)
        share(plan_ref, 2, 1, product, h, m, out_b, 0, h)

    shapes = [(SLOTS, m, cols), (m, cols), (m, cols)]
    product, a, b = small_kernel(body, plan, shapes, [sums[0], swapped], name="return_first")
    return product, [swap_x(a, 0), swap_x(b, 1)]


def near_shares(plan_ref, dz, product, out_a, out_b, from_a, from_b):
    m = product.shape[1]
    h = m // 2
    share(plan_ref, 1, dz, product, 0, h, out_a, 0, m)
    share(plan_ref, 1, dz, product, h, m, out_a, h, m, from_b)
    share(plan_ref, 3, dz, product, 0, h, out_b, 0, m, from_a)
    share(plan_ref, 3, dz, product, h, m, out_b, h, m)


def return_second(plan, product, came):
    _, m, cols = product.shape
    h = m // 2

    def body(plan_ref, ins, outs):
        product, a, b = ins
        out_a, out_b = outs
        part = lambda ref: lambda j: ref[j * h : (j + 1) * h]
        near_shares(plan_ref, 1, product, out_a, out_b, part(a), part(b))
        share(plan_ref, 2, 0, product, 0, h, out_a, 2 * m, h)
        share(plan_ref, 2, 0, product, h, m, out_b, 2 * m, h)

    a, b = small_kernel(
        body, plan, [(3 * m, cols)] * 2, [product, *came], name="return_second"
    )
    return a, [swap_x(a, 0), swap_x(b, 1)]


def return_third(plan, product, came):
    _, m, cols = product.shape
    h = m // 2

    def body(plan_ref, ins, outs):
        product, a, b = ins
        out_a, out_b, across = outs
        part = lambda ref: lambda j: ref[2 * m + j * h : 2 * m + (j + 1) * h]
        near_shares(plan_ref, 0, product, out_a, out_b, part(a), part(b))
        both = lambda j: a[j * m : (j + 1) * m] + b[j * m : (j + 1) * m]
        share(plan_ref, 0, 1, product, 0, m, across, 0, m, both)

    a, b, across = small_kernel(
        body, plan, [(2 * m, cols)] * 3, [product, *came], name="return_third"
    )
    return [swap_x(a, 0), swap_x(b, 1), flip_z(across)]


def return_last(plan, product, came):
    _, m, cols = product.shape

    def body(plan_ref, ins, outs):
        product, *came = ins
        (total,) = outs
        rows = lambda j: slice(j * m, (j + 1) * m)
        arrived = lambda j: came[0][rows(j)] + came[1][rows(j)] + came[2][rows(j)]
        share(plan_ref, 0, 0, product, 0, m, total, 0, m, arrived)

    (total,) = small_kernel(body, plan, [(2 * m, cols)], [product, *came], name="return_last")
    return total


def on_device(amplitudes, labels, integrals):
    flat = labels[:, 0]
    n_tiles = flat.shape[0]
    local_tiles = amplitudes.shape[0] // TILE
    width = amplitudes.shape[1]
    cols = integrals.shape[2]
    row = lax.axis_index("row")
    col = lax.axis_index("col")
    zl, x = row // 4, row % 4
    zh, y, core = col // 8, col // 2 % 4, col % 2

    ids = np.arange(n_tiles, dtype=np.int32)
    same = (flat[:, None] == flat[None, :]) & (ids[None, :] < ids[:, None])
    rank = jnp.sum(same.astype(jnp.int32), axis=1)
    ring = (ids // 2 % 4 - x) * (1 - 2 * (x % 2)) % 4
    place = ring * 4 + ((ids // 8) ^ zl) * 2 + ids % 2
    slot = np.arange(2 * SLOTS, dtype=np.int32)
    target = jnp.where(slot < SLOTS, row, (1 - zl) * 4 + x)
    hit = (flat[None, :] == target[:, None]) & (rank[None, :] == (slot % SLOTS)[:, None])
    wanted = jnp.sum(jnp.where(hit, place[None, :], 0), axis=1)
    held = jnp.where(flat == row, rank, -1)
    slots = jnp.sum(jnp.where(place[None, :] == ids[:, None], held[None, :], 0), axis=1)
    plan = jnp.concatenate([wanted, slots])

    far = flip_core(integrals.reshape(16 * width, cols))
    places = np.arange(8, dtype=np.int32) * 2 + core
    rhs_own = split_rows(integrals.reshape(16 * width, cols), width, places, 0)

    starts = [sum(CHUNKS[:i]) for i in range(len(CHUNKS))]
    whole = [amplitudes, flip_z(amplitudes), swap_x(amplitudes, 0), swap_x(amplitudes, 1)]

    def rows_second(k, *after):
        start, m = starts[k], CHUNKS[k]
        part = lambda a: a.reshape(-1, TILE, width)[:, start : start + m].reshape(-1, width)
        other, *near = wait_for([part(a) for a in whole[1:]], *after)
        return gather_second(near, other, swap_x, local_tiles)[1]

    def rows_third(k, both, *after):
        rows = local_tiles * CHUNKS[k]
        return gather_third(wait_for(both, *after), rows, swap_x, local_tiles)[1]

    rows = [rows_second(0)]
    rows.append(rows_second(1, *rows[0]))
    rows[0] += rows_third(0, rows[0], rhs_own)

    at = []
    for group in GROUPS:
        gz, ring = np.array(group, np.int32).T
        at.append((zh ^ gz) * 4 + (y + ring * (1 - 2 * (y % 2))) % 4)

    def step(group, last):
        m, h = last["m"], last["m"] // 2
        if group == 0:
            arrays, blocks = last["first"], [[(i, 0, m)] for i in range(4)]
        elif group == 1:
            arrays, blocks = last["second"], [[(0, 0, m)], [(1, 0, m)], [(0, m, h), (1, m, h)]]
        else:
            arrays, blocks = last["third"], [[(0, 0, h), (1, 0, h)]]
        where = at[group % 3]
        if group == 3:
            arrays = [*last["second"], *last["third"]]
            blocks = [[(0, 0, m)], [(1, 0, m)], [(0, m, h), (1, m, h)], [(2, 0, h), (3, 0, h)]]
            where = jnp.concatenate(at[1:])
        last["sums"] = products(arrays, blocks, where, rhs, last["sums"])
        return last["sums"]

    def begin(k, *after):
        b, crossing = pick(plan, starts[k], CHUNKS[k], whole + rows[k], after)
        bz = cross_z(crossing)
        return dict(m=SLOTS * CHUNKS[k], sums=[], first=[b, swap_y(b, 0), swap_y(b, 1), bz])

    out, last, back = [], None, None
    this = begin(0)
    rows[1] += rows_third(1, rows[1], this["first"][1])
    rhs = split_rows(far, width, places, 2, rhs_own)
    for k in range(len(CHUNKS)):
        b, *near, bz = this["first"]
        if last is not None:
            near, bz = wait_for((near, bz), last["sums"][0], *last["going"])
        going, this["second"] = gather_second(near, bz, swap_y)
        later = None
        if k + 1 < len(CHUNKS):
            later = begin(k + 1, near[0])
            this["first"] = wait_for(this["first"], later["first"][0])
        if last is not None:
            last["third"] = wait_for(last["third"], *going)
            sums = step(3, last)
            product, came = return_first(plan, sums, flip_core(sums[1]))
            if back is not None:
                out.append(return_last(plan, *back))
        ready = [step(0, this)[0]]
        if last is not None:
            sent, came = return_second(plan, product, wait_for(came, *ready, *out))
            ready.append(sent)
        this["going"], this["third"] = gather_third(wait_for(this["second"], *ready), this["m"], swap_y)
        if later is None:
            sums = step(1, this)
        if last is not None:
            back = product, return_third(plan, product, wait_for(came, sums[0]))
        last, this = this, later
    sums = step(2, last)
    product, came = return_first(plan, sums, flip_core(sums[1]))
    if back is not None:
        out.append(return_last(plan, *back))
    came = return_second(plan, product, wait_for(came, *out))[1]
    out.append(return_last(plan, product, return_third(plan, product, came)))
    out = [o.reshape(local_tiles, -1, cols) for o in out]
    return jnp.concatenate(out, axis=1).reshape(local_tiles * TILE, cols)


def solution(mesh):
    in_specs = (P("row", "col"), P(), P("row", None, "col"))
    out_specs = P("row", "col")
    return jax.shard_map(
        on_device, mesh=mesh, in_specs=in_specs, out_specs=out_specs, check_vma=False
    )
```

```python
import functools

import jax
import jax.numpy as jnp
import numpy as np
from jax import lax
from jax.experimental import pallas as pl
from jax.experimental.pallas import tpu as pltpu
from jax.sharding import PartitionSpec as P

TILE = 128
SLOTS = 4
CHUNKS = (64, 64)

PLACES = [
    (zl, x, zh, y, c)
    for zl in range(2)
    for x in range(4)
    for zh in range(2)
    for y in range(4)
    for c in range(2)
]


def send(a, to):
    index = {p: i for i, p in enumerate(PLACES)}
    return lax.ppermute(a, ("row", "col"), [(i, index[to(*p)]) for p, i in index.items()])


def other_of(i, ring):
    return (i + (1 if i % 2 == ring else 3)) % 4


def swap_x(a, ring):
    return send(a, lambda zl, x, zh, y, c: (zl, other_of(x, ring), zh, y, c))


def swap_y(a, ring):
    return send(a, lambda zl, x, zh, y, c: (zl, x, zh, other_of(y, ring), c))


def flip_z(a):
    return send(a, lambda zl, x, zh, y, c: (1 - zl, x, zh, y, c))


def cross_z(a):
    return send(a, lambda zl, x, zh, y, c: (1 - zl, x, 1 - zh, y, c))


def flip_core(a):
    return send(a, lambda zl, x, zh, y, c: (zl, x, zh, y, 1 - c))


def split(v):
    hi = v.astype(jnp.bfloat16)
    return hi, (v - hi.astype(jnp.float32)).astype(jnp.bfloat16)


def product_kernel(blocks, n_arrays, first, at_ref, *refs):
    arrays, (own_ref, far_ref), refs = refs[:n_arrays], refs[n_arrays : n_arrays + 2], refs[n_arrays + 2 :]
    adds, (out_own, out_far) = refs[:2], refs[-2:]
    step = pl.program_id(0)

    for i, block in enumerate(blocks):

        @pl.when(step == i)
        def _():
            parts = [arrays[array][lo : lo + size] for array, lo, size in block]
            a_hi, a_lo = split(parts[0] if len(parts) == 1 else jnp.concatenate(parts, axis=0))
            a_both = jnp.concatenate([a_hi, a_lo], axis=0)
            m = a_hi.shape[0]
            for j, (rhs, out) in enumerate(((own_ref, out_own), (far_ref, out_far))):
                b_hi, b_lo = split(rhs[...])
                dot = functools.partial(jnp.dot, preferred_element_type=jnp.float32)
                upper = dot(a_both, b_hi)
                term = upper[:m] + (upper[m:] + dot(a_hi, b_lo))
                if i == 0:
                    out[...] = term if first else adds[j][...] + term
                else:
                    out[...] += term


def products(arrays, blocks, at, own, far, sums):
    n = len(blocks)
    m = sum(size for _, _, size in blocks[0])
    width = arrays[0].shape[1]
    cols = own.shape[1]
    vmem = pl.BlockSpec(memory_space=pltpu.VMEM)
    return pl.pallas_call(
        functools.partial(product_kernel, blocks, len(arrays), not sums),
        grid_spec=pltpu.PrefetchScalarGridSpec(
            num_scalar_prefetch=1,
            grid=(n,),
            in_specs=[vmem] * len(arrays)
            + [pl.BlockSpec((width, cols), lambda s, at: (at[s], 0))] * 2
            + [vmem] * len(sums),
            out_specs=[vmem] * 2,
        ),
        out_shape=[jax.ShapeDtypeStruct((m, cols), jnp.float32)] * 2,
        compiler_params=pltpu.CompilerParams(vmem_limit_bytes=50 * 1024 * 1024),
        cost_estimate=pl.CostEstimate(
            flops=12 * n * m * width * cols,
            bytes_accessed=8 * n * width * cols + 4 * n * m * width,
            transcendentals=0,
        ),
        name="products",
    )(at, *arrays, own, far, *sums)


def small_kernel(body, plan, shapes, operands, after=(), name=None):
    def kernel(plan_ref, *refs):
        body(plan_ref, refs[: len(operands)], refs[len(operands) + len(after) :])

    out = pl.pallas_call(
        kernel,
        in_specs=[pl.BlockSpec(memory_space=pltpu.SMEM)]
        + [pl.BlockSpec(memory_space=pltpu.VMEM)] * len(operands)
        + [pl.BlockSpec(memory_space=pl.ANY)] * len(after),
        out_specs=[pl.BlockSpec(memory_space=pltpu.VMEM)] * len(shapes),
        out_shape=[jax.ShapeDtypeStruct(s, jnp.float32) for s in shapes],
        compiler_params=pltpu.CompilerParams(vmem_limit_bytes=24 * 1024 * 1024),
        cost_estimate=pl.CostEstimate(
            flops=0, bytes_accessed=4 * sum(int(np.prod(s)) for s in shapes), transcendentals=0
        ),
        name=name,
    )(plan, *operands, *after)
    return out


def wait_for(value, *others):
    return lax.optimization_barrier((value, others))[0]


def gather_second(near, other, swap, pieces=1):
    return swap(join(other, half(near[1], 0, pieces)), 0), swap(join(other, half(near[0], 1, pieces)), 1)


def gather_third(both, rows, swap, pieces=1):
    return swap(half(both[1][:rows], 0, pieces), 0), swap(half(both[0][:rows], 1, pieces), 1)


def join(*arrays):
    return jnp.concatenate(arrays, axis=0)


def half(a, which, pieces):
    cut = a.reshape(pieces, 2, -1, a.shape[1])[:, which]
    return cut.reshape(-1, a.shape[1])


def pick(plan, m, arrays, after):
    width = arrays[0].shape[1]
    h = m // 2
    where = [
        [(0, 0, m)],
        [(1, 0, m)],
        [(2, 0, m)],
        [(4, 0, m)],
        [(4, 2 * m, h), (5, 2 * m, h)],
        [(6, 0, h), (7, 0, h)],
        [(3, 0, m)],
        [(5, 0, m)],
    ]

    def body(plan_ref, ins, outs):
        for s in range(2 * SLOTS):
            place = plan_ref[s]
            out, to = outs[s // SLOTS], s % SLOTS * m
            for i, parts in enumerate(where):

                @pl.when(place // 2 == i)
                def _():
                    at = to
                    for array, lo, size in parts:
                        rows = pl.ds(pl.multiple_of(lo + place % 2 * size, 8), size)
                        out[at : at + size] = ins[array][rows]
                        at += size

    return small_kernel(body, plan, [(SLOTS * m, width)] * 2, arrays, after, name="pick")


GROUPS = [[(0, 0), (0, 1), (0, 3), (1, 0)], [(1, 1), (1, 3), (0, 2)], [(1, 2)]]


def share(plan_ref, ring, dz, product, lo, hi, out, at, pitch, arrived=None):
    for j in range(2):
        slot = plan_ref[2 * SLOTS + ring * 4 + dz * 2 + j]
        rows = pl.ds(at + j * pitch, hi - lo)

        @pl.when(slot >= 0)
        def _():
            out[rows] = product[slot, lo:hi]

        @pl.when(slot < 0)
        def _():
            if arrived is None:
                out[rows] = jnp.zeros((hi - lo, product.shape[2]), jnp.float32)
            else:
                out[rows] = arrived(j)


def return_first(plan, sums, swapped):
    m, cols = sums[0].shape[0] // SLOTS, sums[0].shape[1]
    h = m // 2

    def body(plan_ref, ins, outs):
        mine, theirs = ins
        product, out_a, out_b = outs
        for s in range(SLOTS):
            rows = slice(s * m, (s + 1) * m)
            product[s] = mine[rows] + theirs[rows]
        share(plan_ref, 2, 1, product, 0, h, out_a, 0, h)
        share(plan_ref, 2, 1, product, h, m, out_b, 0, h)

    shapes = [(SLOTS, m, cols), (m, cols), (m, cols)]
    product, a, b = small_kernel(body, plan, shapes, [sums[0], swapped], name="return_first")
    return product, [swap_x(a, 0), swap_x(b, 1)]


def near_shares(plan_ref, dz, product, out_a, out_b, from_a, from_b):
    m = product.shape[1]
    h = m // 2
    share(plan_ref, 1, dz, product, 0, h, out_a, 0, m)
    share(plan_ref, 1, dz, product, h, m, out_a, h, m, from_b)
    share(plan_ref, 3, dz, product, 0, h, out_b, 0, m, from_a)
    share(plan_ref, 3, dz, product, h, m, out_b, h, m)


def return_second(plan, product, came):
    _, m, cols = product.shape
    h = m // 2

    def body(plan_ref, ins, outs):
        product, a, b = ins
        out_a, out_b = outs
        part = lambda ref: lambda j: ref[j * h : (j + 1) * h]
        near_shares(plan_ref, 1, product, out_a, out_b, part(a), part(b))
        share(plan_ref, 2, 0, product, 0, h, out_a, 2 * m, h)
        share(plan_ref, 2, 0, product, h, m, out_b, 2 * m, h)

    a, b = small_kernel(
        body, plan, [(3 * m, cols)] * 2, [product, *came], name="return_second"
    )
    return a, [swap_x(a, 0), swap_x(b, 1)]


def return_third(plan, product, came):
    _, m, cols = product.shape
    h = m // 2

    def body(plan_ref, ins, outs):
        product, a, b = ins
        out_a, out_b, across = outs
        part = lambda ref: lambda j: ref[2 * m + j * h : 2 * m + (j + 1) * h]
        near_shares(plan_ref, 0, product, out_a, out_b, part(a), part(b))
        both = lambda j: a[j * m : (j + 1) * m] + b[j * m : (j + 1) * m]
        share(plan_ref, 0, 1, product, 0, m, across, 0, m, both)

    a, b, across = small_kernel(
        body, plan, [(2 * m, cols)] * 3, [product, *came], name="return_third"
    )
    return [swap_x(a, 0), swap_x(b, 1), flip_z(across)]


def return_last(plan, product, came):
    _, m, cols = product.shape

    def body(plan_ref, ins, outs):
        product, *came = ins
        (total,) = outs
        rows = lambda j: slice(j * m, (j + 1) * m)
        arrived = lambda j: came[0][rows(j)] + came[1][rows(j)] + came[2][rows(j)]
        share(plan_ref, 0, 0, product, 0, m, total, 0, m, arrived)

    (total,) = small_kernel(body, plan, [(2 * m, cols)], [product, *came], name="return_last")
    return total


def on_device(amplitudes, labels, integrals):
    flat = labels[:, 0]
    n_tiles = flat.shape[0]
    local_tiles = amplitudes.shape[0] // TILE
    width = amplitudes.shape[1]
    cols = integrals.shape[2]
    row = lax.axis_index("row")
    col = lax.axis_index("col")
    zl, x = row // 4, row % 4
    zh, y, core = col // 8, col // 2 % 4, col % 2

    ids = np.arange(n_tiles, dtype=np.int32)
    same = (flat[:, None] == flat[None, :]) & (ids[None, :] < ids[:, None])
    rank = jnp.sum(same.astype(jnp.int32), axis=1)
    ring = (ids // 2 % 4 - x) * (1 - 2 * (x % 2)) % 4
    place = ring * 4 + ((ids // 8) ^ zl) * 2 + ids % 2
    slot = np.arange(2 * SLOTS, dtype=np.int32)
    target = jnp.where(slot < SLOTS, row, (1 - zl) * 4 + x)
    hit = (flat[None, :] == target[:, None]) & (rank[None, :] == (slot % SLOTS)[:, None])
    wanted = jnp.sum(jnp.where(hit, place[None, :], 0), axis=1)
    held = jnp.where(flat == row, rank, -1)
    slots = jnp.sum(jnp.where(place[None, :] == ids[:, None], held[None, :], 0), axis=1)
    plan = jnp.concatenate([wanted, slots])

    tiles = amplitudes.reshape(local_tiles, TILE, width)
    starts = [sum(CHUNKS[:i]) for i in range(len(CHUNKS))]
    pieces = [tiles[:, s : s + m].reshape(-1, width) for s, m in zip(starts, CHUNKS)]

    own = integrals.reshape(16 * width, cols)
    far = flip_core(own)
    at = []
    for group in GROUPS:
        gz, ring = np.array(group, np.int32).T
        places = (zh ^ gz) * 4 + (y + ring * (1 - 2 * (y % 2))) % 4
        at.append(places * 2 + core)

    def rows_first(piece, before=None):
        beside, later = (), ()
        if before is not None:
            beside, later = before[1:4], before[4:6]
        other = flip_z(wait_for(piece, *beside))
        own = wait_for(piece, *later)
        return [piece, other, swap_x(own, 0), swap_x(own, 1)]

    def rows_second(arrays):
        return arrays + list(gather_second(arrays[2:4], arrays[1], swap_x, local_tiles))

    def rows_third(arrays):
        rows = arrays[1].shape[0]
        return arrays + list(gather_third(arrays[4:6], rows, swap_x, local_tiles))

    def step(group, last):
        m, h = last["m"], last["m"] // 2
        if group == 0:
            arrays, blocks = last["first"], [[(i, 0, m)] for i in range(4)]
        elif group == 1:
            arrays, blocks = last["second"], [[(0, 0, m)], [(1, 0, m)], [(0, m, h), (1, m, h)]]
        else:
            arrays, blocks = last["third"], [[(0, 0, h), (1, 0, h)]]
        last["sums"] = products(arrays, blocks, at[group], own, far, last["sums"])
        return last["sums"]

    def finish(last, back):
        sums = step(1, last)
        if back is not None:
            product, came = back
            back = product, return_third(plan, product, wait_for(came, sums[0]))
        return step(2, last), back

    arrays = rows_third(rows_second(rows_first(pieces[0])))
    out, last, back = [], None, None
    for k, m in enumerate(CHUNKS):
        more = k + 1 < len(CHUNKS)
        after = () if last is None else (last["second"][0], last["sums"][0])
        b, crossing = pick(plan, m, arrays, after)
        this = dict(m=SLOTS * m, sums=[])
        if more:
            arrays = rows_first(pieces[k + 1], arrays)
        near = [swap_y(b, 0), swap_y(b, 1)]
        bz = cross_z(crossing)
        this["first"] = [b, *near, bz]
        ready = []
        if last is not None:
            sums, back = finish(last, back)
            swapped = flip_core(sums[1])
            ready = [*ready, sums[0]]
        near, bz = wait_for((near, bz), *ready)
        this["second"] = gather_second(near, bz, swap_y)
        if more:
            arrays = rows_second(wait_for(arrays, near[0]))
        ready = arrays[4:6] if more else []
        if last is not None:
            product, came = return_first(plan, sums, swapped)
        step(0, this)
        if last is not None:
            if back is not None:
                out.append(return_last(plan, *back))
            sent, came = return_second(plan, product, wait_for(came, this["sums"][0], *out))
            back = product, came
            ready = [*ready, sent]
        both = wait_for(this["second"], this["sums"][0], *ready)
        this["third"] = gather_third(both, SLOTS * m, swap_y)
        if more:
            arrays = rows_third(wait_for(arrays, this["sums"][0]))
        last = this
    sums, back = finish(last, back)
    product, came = return_first(plan, sums, flip_core(sums[1]))
    if back is not None:
        out.append(return_last(plan, *back))
    came = return_second(plan, product, wait_for(came, *out))[1]
    out.append(return_last(plan, product, return_third(plan, product, came)))
    out = [o.reshape(local_tiles, -1, cols) for o in out]
    return jnp.concatenate(out, axis=1).reshape(local_tiles * TILE, cols)


def solution(mesh):
    in_specs = (P("row", "col"), P(), P("row", None, "col"))
    out_specs = P("row", "col")
    return jax.shard_map(
        on_device, mesh=mesh, in_specs=in_specs, out_specs=out_specs, check_vma=False
    )
```

```python
import functools

import jax
import jax.numpy as jnp
import numpy as np
from jax import lax
from jax.experimental import pallas as pl
from jax.experimental.pallas import tpu as pltpu
from jax.sharding import PartitionSpec as P

TILE = 128
SLOTS = 4
CHUNKS = (64, 64)
SPLIT_MIB = 40
PRODUCTS_MIB = 16
SMALL_MIB = 8

PLACES = [
    (zl, x, zh, y, c)
    for zl in range(2)
    for x in range(4)
    for zh in range(2)
    for y in range(4)
    for c in range(2)
]


def send(a, to):
    index = {p: i for i, p in enumerate(PLACES)}
    return lax.ppermute(a, ("row", "col"), [(i, index[to(*p)]) for p, i in index.items()])


def other_of(i, ring):
    return (i + (1 if i % 2 == ring else 3)) % 4


def swap_x(a, ring):
    return send(a, lambda zl, x, zh, y, c: (zl, other_of(x, ring), zh, y, c))


def swap_y(a, ring):
    return send(a, lambda zl, x, zh, y, c: (zl, x, zh, other_of(y, ring), c))


def flip_z(a):
    return send(a, lambda zl, x, zh, y, c: (1 - zl, x, zh, y, c))


def cross_z(a):
    return send(a, lambda zl, x, zh, y, c: (1 - zl, x, 1 - zh, y, c))


def flip_core(a):
    return send(a, lambda zl, x, zh, y, c: (zl, x, zh, y, 1 - c))


def split(v):
    hi = v.astype(jnp.bfloat16)
    return hi, (v - hi.astype(jnp.float32)).astype(jnp.bfloat16)


def split_rows(a, width, at, name):
    n, cols = at.shape[0], a.shape[1]

    def kernel(at_ref, a_ref, hi_ref, lo_ref):
        rows = pl.ds(pl.multiple_of(pl.program_id(0) * width, width), width)
        hi_ref[rows], lo_ref[rows] = split(a_ref[...])

    return pl.pallas_call(
        kernel,
        grid_spec=pltpu.PrefetchScalarGridSpec(
            num_scalar_prefetch=1,
            grid=(n,),
            in_specs=[pl.BlockSpec((width, cols), lambda s, at: (at[s], 0))],
            out_specs=[pl.BlockSpec(memory_space=pltpu.VMEM)] * 2,
        ),
        out_shape=[jax.ShapeDtypeStruct((n * width, cols), jnp.bfloat16)] * 2,
        compiler_params=pltpu.CompilerParams(vmem_limit_bytes=SPLIT_MIB * 1024 * 1024),
        name=name,
    )(at, a)


def products(arrays, blocks, at, rhs, sums):
    n = len(blocks)
    m = sum(size for _, _, size in blocks[0])
    width = arrays[0].shape[1]
    cols = rhs[0].shape[1]
    dot = functools.partial(jnp.dot, preferred_element_type=jnp.float32)

    def kernel(at_ref, *refs):
        ins, refs = refs[: len(arrays)], refs[len(arrays) :]
        parts, adds, outs = refs[:4], refs[4:-2], refs[-2:]
        for i, block in enumerate(blocks):
            rows = [ins[array][lo : lo + size] for array, lo, size in block]
            a_hi, a_lo = split(rows[0] if len(rows) == 1 else jnp.concatenate(rows, axis=0))
            a_both = jnp.concatenate([a_hi, a_lo], axis=0)
            deep = pl.ds(pl.multiple_of(at_ref[i] * width, width), width)
            for j, out in enumerate(outs):
                upper = dot(a_both, parts[2 * j][deep])
                term = upper[:m] + (upper[m:] + dot(a_hi, parts[2 * j + 1][deep]))
                if i == 0:
                    out[...] = adds[j][...] + term if sums else term
                else:
                    out[...] += term

    vmem = pl.BlockSpec(memory_space=pltpu.VMEM)
    return pl.pallas_call(
        kernel,
        in_specs=[pl.BlockSpec(memory_space=pltpu.SMEM)]
        + [vmem] * (len(arrays) + 4 + len(sums)),
        out_specs=[vmem] * 2,
        out_shape=[jax.ShapeDtypeStruct((m, cols), jnp.float32)] * 2,
        compiler_params=pltpu.CompilerParams(vmem_limit_bytes=PRODUCTS_MIB * 1024 * 1024),
        cost_estimate=pl.CostEstimate(
            flops=12 * n * m * width * cols,
            bytes_accessed=8 * n * width * cols + 4 * n * m * width,
            transcendentals=0,
        ),
        name="products",
    )(at, *arrays, *rhs, *sums)


def small_kernel(body, plan, shapes, operands, after=(), name=None):
    def kernel(plan_ref, *refs):
        body(plan_ref, refs[: len(operands)], refs[len(operands) + len(after) :])

    out = pl.pallas_call(
        kernel,
        in_specs=[pl.BlockSpec(memory_space=pltpu.SMEM)]
        + [pl.BlockSpec(memory_space=pltpu.VMEM)] * len(operands)
        + [pl.BlockSpec(memory_space=pl.ANY)] * len(after),
        out_specs=[pl.BlockSpec(memory_space=pltpu.VMEM)] * len(shapes),
        out_shape=[jax.ShapeDtypeStruct(s, jnp.float32) for s in shapes],
        compiler_params=pltpu.CompilerParams(vmem_limit_bytes=SMALL_MIB * 1024 * 1024),
        cost_estimate=pl.CostEstimate(
            flops=0, bytes_accessed=4 * sum(int(np.prod(s)) for s in shapes), transcendentals=0
        ),
        name=name,
    )(plan, *operands, *after)
    return out


def wait_for(value, *others):
    return lax.optimization_barrier((value, others))[0]


def gather_second(near, other, swap, pieces=1):
    return swap(join(other, half(near[1], 0, pieces)), 0), swap(join(other, half(near[0], 1, pieces)), 1)


def gather_third(both, rows, swap, pieces=1):
    return swap(half(both[1][:rows], 0, pieces), 0), swap(half(both[0][:rows], 1, pieces), 1)


def join(*arrays):
    return jnp.concatenate(arrays, axis=0)


def half(a, which, pieces):
    cut = a.reshape(pieces, 2, -1, a.shape[1])[:, which]
    return cut.reshape(-1, a.shape[1])


def pick(plan, m, arrays, after):
    width = arrays[0].shape[1]
    h = m // 2
    where = [
        [(0, 0, m)],
        [(1, 0, m)],
        [(2, 0, m)],
        [(4, 0, m)],
        [(4, 2 * m, h), (5, 2 * m, h)],
        [(6, 0, h), (7, 0, h)],
        [(3, 0, m)],
        [(5, 0, m)],
    ]

    def body(plan_ref, ins, outs):
        for s in range(2 * SLOTS):
            place = plan_ref[s]
            out, to = outs[s // SLOTS], s % SLOTS * m
            for i, parts in enumerate(where):

                @pl.when(place // 2 == i)
                def _():
                    at = to
                    for array, lo, size in parts:
                        rows = pl.ds(pl.multiple_of(lo + place % 2 * size, 8), size)
                        out[at : at + size] = ins[array][rows]
                        at += size

    return small_kernel(body, plan, [(SLOTS * m, width)] * 2, arrays, after, name="pick")


GROUPS = [[(0, 0), (0, 1), (0, 3), (1, 0)], [(1, 1), (1, 3), (0, 2)], [(1, 2)]]


def share(plan_ref, ring, dz, product, lo, hi, out, at, pitch, arrived=None):
    for j in range(2):
        slot = plan_ref[2 * SLOTS + ring * 4 + dz * 2 + j]
        rows = pl.ds(at + j * pitch, hi - lo)

        @pl.when(slot >= 0)
        def _():
            out[rows] = product[slot, lo:hi]

        @pl.when(slot < 0)
        def _():
            if arrived is None:
                out[rows] = jnp.zeros((hi - lo, product.shape[2]), jnp.float32)
            else:
                out[rows] = arrived(j)


def return_first(plan, sums, swapped):
    m, cols = sums[0].shape[0] // SLOTS, sums[0].shape[1]
    h = m // 2

    def body(plan_ref, ins, outs):
        mine, theirs = ins
        product, out_a, out_b = outs
        for s in range(SLOTS):
            rows = slice(s * m, (s + 1) * m)
            product[s] = mine[rows] + theirs[rows]
        share(plan_ref, 2, 1, product, 0, h, out_a, 0, h)
        share(plan_ref, 2, 1, product, h, m, out_b, 0, h)

    shapes = [(SLOTS, m, cols), (m, cols), (m, cols)]
    product, a, b = small_kernel(body, plan, shapes, [sums[0], swapped], name="return_first")
    return product, [swap_x(a, 0), swap_x(b, 1)]


def near_shares(plan_ref, dz, product, out_a, out_b, from_a, from_b):
    m = product.shape[1]
    h = m // 2
    share(plan_ref, 1, dz, product, 0, h, out_a, 0, m)
    share(plan_ref, 1, dz, product, h, m, out_a, h, m, from_b)
    share(plan_ref, 3, dz, product, 0, h, out_b, 0, m, from_a)
    share(plan_ref, 3, dz, product, h, m, out_b, h, m)


def return_second(plan, product, came):
    _, m, cols = product.shape
    h = m // 2

    def body(plan_ref, ins, outs):
        product, a, b = ins
        out_a, out_b = outs
        part = lambda ref: lambda j: ref[j * h : (j + 1) * h]
        near_shares(plan_ref, 1, product, out_a, out_b, part(a), part(b))
        share(plan_ref, 2, 0, product, 0, h, out_a, 2 * m, h)
        share(plan_ref, 2, 0, product, h, m, out_b, 2 * m, h)

    a, b = small_kernel(
        body, plan, [(3 * m, cols)] * 2, [product, *came], name="return_second"
    )
    return a, [swap_x(a, 0), swap_x(b, 1)]


def return_third(plan, product, came):
    _, m, cols = product.shape
    h = m // 2

    def body(plan_ref, ins, outs):
        product, a, b = ins
        out_a, out_b, across = outs
        part = lambda ref: lambda j: ref[2 * m + j * h : 2 * m + (j + 1) * h]
        near_shares(plan_ref, 0, product, out_a, out_b, part(a), part(b))
        both = lambda j: a[j * m : (j + 1) * m] + b[j * m : (j + 1) * m]
        share(plan_ref, 0, 1, product, 0, m, across, 0, m, both)

    a, b, across = small_kernel(
        body, plan, [(2 * m, cols)] * 3, [product, *came], name="return_third"
    )
    return across, [swap_x(a, 0), swap_x(b, 1), flip_z(across)]


def return_last(plan, product, came, earlier=None):
    _, m, cols = product.shape
    start = 0 if earlier is None else earlier.shape[0] // 2
    pitch = start + m

    def body(plan_ref, ins, outs):
        product, a, b, c, *before = ins
        (total,) = outs
        rows = lambda j: slice(j * m, (j + 1) * m)
        arrived = lambda j: a[rows(j)] + b[rows(j)] + c[rows(j)]
        share(plan_ref, 0, 0, product, 0, m, total, start, pitch, arrived)
        for j in range(2 if before else 0):
            total[j * pitch : j * pitch + start] = before[0][j * start : (j + 1) * start]

    before = [] if earlier is None else [earlier]
    (total,) = small_kernel(
        body, plan, [(2 * pitch, cols)], [product, *came, *before], name="return_last"
    )
    return total


def on_device(amplitudes, labels, integrals):
    flat = labels[:, 0]
    n_tiles = flat.shape[0]
    local_tiles = amplitudes.shape[0] // TILE
    width = amplitudes.shape[1]
    cols = integrals.shape[2]
    row = lax.axis_index("row")
    col = lax.axis_index("col")
    zl, x = row // 4, row % 4
    zh, y, core = col // 8, col // 2 % 4, col % 2

    ids = np.arange(n_tiles, dtype=np.int32)
    same = (flat[:, None] == flat[None, :]) & (ids[None, :] < ids[:, None])
    rank = jnp.sum(same.astype(jnp.int32), axis=1)
    ring = (ids // 2 % 4 - x) * (1 - 2 * (x % 2)) % 4
    place = ring * 4 + ((ids // 8) ^ zl) * 2 + ids % 2
    slot = np.arange(2 * SLOTS, dtype=np.int32)
    target = jnp.where(slot < SLOTS, row, (1 - zl) * 4 + x)
    hit = (flat[None, :] == target[:, None]) & (rank[None, :] == (slot % SLOTS)[:, None])
    wanted = jnp.sum(jnp.where(hit, place[None, :], 0), axis=1)
    held = jnp.where(flat == row, rank, -1)
    slots = jnp.sum(jnp.where(place[None, :] == ids[:, None], held[None, :], 0), axis=1)
    plan = jnp.concatenate([wanted, slots])

    tiles = amplitudes.reshape(local_tiles, TILE, width)
    starts = [sum(CHUNKS[:i]) for i in range(len(CHUNKS))]
    pieces = [tiles[:, s : s + m].reshape(-1, width) for s, m in zip(starts, CHUNKS)]

    own = integrals.reshape(16 * width, cols)
    far = flip_core(own)
    deep = np.arange(8, dtype=np.int32) * 2 + core
    rhs_own = split_rows(own, width, deep, "split_own")
    rhs_far = split_rows(far, width, deep, "split_far")
    rhs = [*rhs_own, *rhs_far]
    at = []
    for group in GROUPS:
        gz, ring = np.array(group, np.int32).T
        places = (zh ^ gz) * 4 + (y + ring * (1 - 2 * (y % 2))) % 4
        at.append(places)

    def rows_first(piece, before=None):
        beside, later = (), ()
        if before is not None:
            beside, later = before[1:4], before[4:6]
        other = flip_z(wait_for(piece, *beside))
        own = wait_for(piece, *later)
        return [piece, other, swap_x(own, 0), swap_x(own, 1)]

    def rows_second(arrays):
        return arrays + list(gather_second(arrays[2:4], arrays[1], swap_x, local_tiles))

    def rows_third(arrays):
        rows = arrays[1].shape[0]
        return arrays + list(gather_third(arrays[4:6], rows, swap_x, local_tiles))

    def step(group, last):
        m, h = last["m"], last["m"] // 2
        if group == 0:
            arrays, blocks = last["first"], [[(i, 0, m)] for i in range(4)]
        elif group == 1:
            arrays, blocks = last["second"], [[(0, 0, m)], [(1, 0, m)], [(0, m, h), (1, m, h)]]
        else:
            arrays, blocks = last["third"], [[(0, 0, h), (1, 0, h)]]
        last["sums"] = products(arrays, blocks, at[group], rhs, last["sums"])
        return last["sums"]

    def finish(last, back):
        sums = step(1, last)
        if back is not None:
            product, came = back
            sent, came = return_third(plan, product, wait_for(came, sums[0]))
            last["sums"] = wait_for(sums, sent)
            back = product, came
        return step(2, last), back

    arrays = rows_third(wait_for(rows_second(rows_first(pieces[0])), rhs_own[0]))
    last, back = None, None
    for k, m in enumerate(CHUNKS):
        more = k + 1 < len(CHUNKS)
        after = () if last is None else (last["second"][0], last["sums"][0])
        b, crossing = pick(plan, m, arrays, after)
        this = dict(m=SLOTS * m, sums=[])
        if more:
            arrays = rows_first(pieces[k + 1], arrays)
        near = [swap_y(b, 0), swap_y(b, 1)]
        bz = cross_z(crossing)
        this["first"] = [b, *near, bz]
        ready = [] if k else rhs_far[:1]
        if last is not None:
            sums, back = finish(last, back)
            swapped = flip_core(sums[1])
            ready = [*ready, sums[0]]
        near, bz = wait_for((near, bz), *ready)
        this["second"] = gather_second(near, bz, swap_y)
        if more:
            arrays = rows_second(wait_for(arrays, near[0]))
        ready = arrays[4:6] if more else []
        if last is not None:
            product, came = return_first(plan, sums, swapped)
        step(0, this)
        if last is not None:
            sent, came = return_second(plan, product, wait_for(came, this["sums"][0]))
            back = product, came
            ready = [*ready, *came]
        both = wait_for(this["second"], this["sums"][0], *ready)
        this["third"] = gather_third(both, SLOTS * m, swap_y)
        if more:
            arrays = rows_third(wait_for(arrays, this["sums"][0]))
        last = this
    sums, back = finish(last, back)
    product, came = return_first(plan, sums, flip_core(sums[1]))
    result = return_last(plan, *back)
    came = return_second(plan, product, wait_for(came, result))[1]
    return return_last(plan, product, return_third(plan, product, came)[1], result)


def solution(mesh):
    in_specs = (P("row", "col"), P(), P("row", None, "col"))
    out_specs = P("row", "col")
    return jax.shard_map(
        on_device, mesh=mesh, in_specs=in_specs, out_specs=out_specs, check_vma=False
    )
```

```python
import functools

import jax
import jax.numpy as jnp
import numpy as np
from jax import lax
from jax.experimental import pallas as pl
from jax.experimental.pallas import tpu as pltpu
from jax.sharding import PartitionSpec as P

TILE = 128
SLOTS = 4
CHUNKS = (64, 64)
BRIEF = pl.CostEstimate(flops=1, bytes_accessed=1, transcendentals=0)

PLACES = [
    (zl, x, zh, y, c)
    for zl in range(2)
    for x in range(4)
    for zh in range(2)
    for y in range(4)
    for c in range(2)
]


def send(a, to):
    index = {p: i for i, p in enumerate(PLACES)}
    return lax.ppermute(a, ("row", "col"), [(i, index[to(*p)]) for p, i in index.items()])


def other_of(i, ring):
    return (i + (1 if i % 2 == ring else 3)) % 4


def swap_x(a, ring):
    return send(a, lambda zl, x, zh, y, c: (zl, other_of(x, ring), zh, y, c))


def swap_y(a, ring):
    return send(a, lambda zl, x, zh, y, c: (zl, x, zh, other_of(y, ring), c))


def flip_z(a):
    return send(a, lambda zl, x, zh, y, c: (1 - zl, x, zh, y, c))


def cross_z(a):
    return send(a, lambda zl, x, zh, y, c: (1 - zl, x, 1 - zh, y, c))


def flip_core(a):
    return send(a, lambda zl, x, zh, y, c: (zl, x, zh, y, 1 - c))


def split(v):
    hi = v.astype(jnp.bfloat16)
    return hi, (v - hi.astype(jnp.float32)).astype(jnp.bfloat16)


def product_kernel(blocks, n_arrays, first, at_ref, *refs):
    arrays, (own_ref, far_ref), refs = refs[:n_arrays], refs[n_arrays : n_arrays + 2], refs[n_arrays + 2 :]
    adds, (out_own, out_far) = refs[:2], refs[-2:]
    step = pl.program_id(0)

    for i, block in enumerate(blocks):

        @pl.when(step == i)
        def _():
            parts = [arrays[array][lo : lo + size] for array, lo, size in block]
            a_hi, a_lo = split(parts[0] if len(parts) == 1 else jnp.concatenate(parts, axis=0))
            a_both = jnp.concatenate([a_hi, a_lo], axis=0)
            m = a_hi.shape[0]
            for j, (rhs, out) in enumerate(((own_ref, out_own), (far_ref, out_far))):
                b_hi, b_lo = split(rhs[...])
                dot = functools.partial(jnp.dot, preferred_element_type=jnp.float32)
                upper = dot(a_both, b_hi)
                term = upper[:m] + (upper[m:] + dot(a_hi, b_lo))
                if i == 0:
                    out[...] = term if first else adds[j][...] + term
                else:
                    out[...] += term


def products(arrays, blocks, at, own, far, sums):
    n = len(blocks)
    m = sum(size for _, _, size in blocks[0])
    width = arrays[0].shape[1]
    cols = own.shape[1]
    vmem = pl.BlockSpec(memory_space=pltpu.VMEM)
    return pl.pallas_call(
        functools.partial(product_kernel, blocks, len(arrays), not sums),
        grid_spec=pltpu.PrefetchScalarGridSpec(
            num_scalar_prefetch=1,
            grid=(n,),
            in_specs=[vmem] * len(arrays)
            + [pl.BlockSpec((width, cols), lambda s, at: (at[s], 0))] * 2
            + [vmem] * len(sums),
            out_specs=[vmem] * 2,
        ),
        out_shape=[jax.ShapeDtypeStruct((m, cols), jnp.float32)] * 2,
        compiler_params=pltpu.CompilerParams(vmem_limit_bytes=50 * 1024 * 1024),
        cost_estimate=BRIEF,
        name="products",
    )(at, *arrays, own, far, *sums)


def small_kernel(body, plan, shapes, operands, after=(), name=None):
    def kernel(plan_ref, *refs):
        body(plan_ref, refs[: len(operands)], refs[len(operands) + len(after) :])

    out = pl.pallas_call(
        kernel,
        in_specs=[pl.BlockSpec(memory_space=pltpu.SMEM)]
        + [pl.BlockSpec(memory_space=pltpu.VMEM)] * len(operands)
        + [pl.BlockSpec(memory_space=pl.ANY)] * len(after),
        out_specs=[pl.BlockSpec(memory_space=pltpu.VMEM)] * len(shapes),
        out_shape=[jax.ShapeDtypeStruct(s, jnp.float32) for s in shapes],
        compiler_params=pltpu.CompilerParams(vmem_limit_bytes=24 * 1024 * 1024),
        cost_estimate=pl.CostEstimate(
            flops=0, bytes_accessed=4 * sum(int(np.prod(s)) for s in shapes), transcendentals=0
        ),
        name=name,
    )(plan, *operands, *after)
    return out


def wait_for(value, *others):
    return lax.optimization_barrier((value, others))[0]


def gather_second(near, other, swap, pieces=1):
    going = [join(other, half(near[1 - i], i, pieces)) for i in range(2)]
    return going, [swap(a, i) for i, a in enumerate(going)]


def gather_third(both, rows, swap, pieces=1):
    return swap(half(both[1][:rows], 0, pieces), 0), swap(half(both[0][:rows], 1, pieces), 1)


def join(*arrays):
    return jnp.concatenate(arrays, axis=0)


def half(a, which, pieces):
    cut = a.reshape(pieces, 2, -1, a.shape[1])[:, which]
    return cut.reshape(-1, a.shape[1])


def pick(plan, m, arrays, after):
    width = arrays[0].shape[1]
    h = m // 2
    where = [
        [(0, 0, m)],
        [(1, 0, m)],
        [(2, 0, m)],
        [(4, 0, m)],
        [(4, 2 * m, h), (5, 2 * m, h)],
        [(6, 0, h), (7, 0, h)],
        [(3, 0, m)],
        [(5, 0, m)],
    ]

    def body(plan_ref, ins, outs):
        for s in range(2 * SLOTS):
            place = plan_ref[s]
            out, to = outs[s // SLOTS], s % SLOTS * m
            for i, parts in enumerate(where):

                @pl.when(place // 2 == i)
                def _():
                    at = to
                    for array, lo, size in parts:
                        rows = pl.ds(pl.multiple_of(lo + place % 2 * size, 8), size)
                        out[at : at + size] = ins[array][rows]
                        at += size

    return small_kernel(body, plan, [(SLOTS * m, width)] * 2, arrays, after, name="pick")


GROUPS = [[(0, 0), (0, 1), (0, 3), (1, 0)], [(1, 1), (1, 3), (0, 2)], [(1, 2)]]


def share(plan_ref, ring, dz, product, lo, hi, out, at, pitch, arrived=None):
    for j in range(2):
        slot = plan_ref[2 * SLOTS + ring * 4 + dz * 2 + j]
        rows = pl.ds(at + j * pitch, hi - lo)

        @pl.when(slot >= 0)
        def _():
            out[rows] = product[slot, lo:hi]

        @pl.when(slot < 0)
        def _():
            if arrived is None:
                out[rows] = jnp.zeros((hi - lo, product.shape[2]), jnp.float32)
            else:
                out[rows] = arrived(j)


def return_first(plan, sums, swapped):
    m, cols = sums[0].shape[0] // SLOTS, sums[0].shape[1]
    h = m // 2

    def body(plan_ref, ins, outs):
        mine, theirs = ins
        product, out_a, out_b = outs
        for s in range(SLOTS):
            rows = slice(s * m, (s + 1) * m)
            product[s] = mine[rows] + theirs[rows]
        share(plan_ref, 2, 1, product, 0, h, out_a, 0, h)
        share(plan_ref, 2, 1, product, h, m, out_b, 0, h)

    shapes = [(SLOTS, m, cols), (m, cols), (m, cols)]
    product, a, b = small_kernel(body, plan, shapes, [sums[0], swapped], name="return_first")
    return product, [swap_x(a, 0), swap_x(b, 1)]


def near_shares(plan_ref, dz, product, out_a, out_b, from_a, from_b):
    m = product.shape[1]
    h = m // 2
    share(plan_ref, 1, dz, product, 0, h, out_a, 0, m)
    share(plan_ref, 1, dz, product, h, m, out_a, h, m, from_b)
    share(plan_ref, 3, dz, product, 0, h, out_b, 0, m, from_a)
    share(plan_ref, 3, dz, product, h, m, out_b, h, m)


def return_second(plan, product, came):
    _, m, cols = product.shape
    h = m // 2

    def body(plan_ref, ins, outs):
        product, a, b = ins
        out_a, out_b = outs
        part = lambda ref: lambda j: ref[j * h : (j + 1) * h]
        near_shares(plan_ref, 1, product, out_a, out_b, part(a), part(b))
        share(plan_ref, 2, 0, product, 0, h, out_a, 2 * m, h)
        share(plan_ref, 2, 0, product, h, m, out_b, 2 * m, h)

    a, b = small_kernel(
        body, plan, [(3 * m, cols)] * 2, [product, *came], name="return_second"
    )
    return a, [swap_x(a, 0), swap_x(b, 1)]


def return_third(plan, product, came):
    _, m, cols = product.shape
    h = m // 2

    def body(plan_ref, ins, outs):
        product, a, b = ins
        out_a, out_b, across = outs
        part = lambda ref: lambda j: ref[2 * m + j * h : 2 * m + (j + 1) * h]
        near_shares(plan_ref, 0, product, out_a, out_b, part(a), part(b))
        both = lambda j: a[j * m : (j + 1) * m] + b[j * m : (j + 1) * m]
        share(plan_ref, 0, 1, product, 0, m, across, 0, m, both)

    a, b, across = small_kernel(
        body, plan, [(2 * m, cols)] * 3, [product, *came], name="return_third"
    )
    return [swap_x(a, 0), swap_x(b, 1), flip_z(across)]


def return_last(plan, product, came):
    _, m, cols = product.shape

    def body(plan_ref, ins, outs):
        product, *came = ins
        (total,) = outs
        rows = lambda j: slice(j * m, (j + 1) * m)
        arrived = lambda j: came[0][rows(j)] + came[1][rows(j)] + came[2][rows(j)]
        share(plan_ref, 0, 0, product, 0, m, total, 0, m, arrived)

    (total,) = small_kernel(body, plan, [(2 * m, cols)], [product, *came], name="return_last")
    return total


def on_device(amplitudes, labels, integrals):
    flat = labels[:, 0]
    n_tiles = flat.shape[0]
    local_tiles = amplitudes.shape[0] // TILE
    width = amplitudes.shape[1]
    cols = integrals.shape[2]
    row = lax.axis_index("row")
    col = lax.axis_index("col")
    zl, x = row // 4, row % 4
    zh, y, core = col // 8, col // 2 % 4, col % 2

    ids = np.arange(n_tiles, dtype=np.int32)
    same = (flat[:, None] == flat[None, :]) & (ids[None, :] < ids[:, None])
    rank = jnp.sum(same.astype(jnp.int32), axis=1)
    ring = (ids // 2 % 4 - x) * (1 - 2 * (x % 2)) % 4
    place = ring * 4 + ((ids // 8) ^ zl) * 2 + ids % 2
    slot = np.arange(2 * SLOTS, dtype=np.int32)
    target = jnp.where(slot < SLOTS, row, (1 - zl) * 4 + x)
    hit = (flat[None, :] == target[:, None]) & (rank[None, :] == (slot % SLOTS)[:, None])
    wanted = jnp.sum(jnp.where(hit, place[None, :], 0), axis=1)
    held = jnp.where(flat == row, rank, -1)
    slots = jnp.sum(jnp.where(place[None, :] == ids[:, None], held[None, :], 0), axis=1)
    plan = jnp.concatenate([wanted, slots])

    tiles = amplitudes.reshape(local_tiles, TILE, width)
    starts = [sum(CHUNKS[:i]) for i in range(len(CHUNKS))]
    pieces = [tiles[:, s : s + m].reshape(-1, width) for s, m in zip(starts, CHUNKS)]

    own = integrals.reshape(16 * width, cols)
    far = flip_core(own)
    at = []
    for group in GROUPS:
        gz, ring = np.array(group, np.int32).T
        places = (zh ^ gz) * 4 + (y + ring * (1 - 2 * (y % 2))) % 4
        at.append(places * 2 + core)

    def rows_first(piece, before=None):
        beside, later = (), ()
        if before is not None:
            beside, later = before[1:4], before[4:6]
        other = flip_z(wait_for(piece, *beside))
        own = wait_for(piece, *later)
        return [piece, other, swap_x(own, 0), swap_x(own, 1)]

    def rows_second(arrays):
        return arrays + gather_second(arrays[2:4], arrays[1], swap_x, local_tiles)[1]

    def rows_third(arrays):
        rows = arrays[1].shape[0]
        return arrays + list(gather_third(arrays[4:6], rows, swap_x, local_tiles))

    def step(group, last):
        m, h = last["m"], last["m"] // 2
        if group == 0:
            arrays, blocks = last["first"], [[(i, 0, m)] for i in range(4)]
        elif group == 1:
            arrays, blocks = last["second"], [[(0, 0, m)], [(1, 0, m)], [(0, m, h), (1, m, h)]]
        else:
            arrays, blocks = last["third"], [[(0, 0, h), (1, 0, h)]]
        last["sums"] = products(arrays, blocks, at[group], own, far, last["sums"])
        return last["sums"]

    def finish(last, back):
        sums = step(1, last)
        if back is not None:
            product, came = back
            back = product, return_third(plan, product, wait_for(came, sums[0]))
        return step(2, last), back

    arrays = rows_third(rows_second(rows_first(pieces[0])))
    out, last, back = [], None, None
    for k, m in enumerate(CHUNKS):
        more = k + 1 < len(CHUNKS)
        after = () if last is None else (last["second"][0], last["sums"][0])
        if more:
            later = rows_first(pieces[k + 1], arrays)
            after = (*after, later[1])
        b, crossing = pick(plan, m, arrays, after)
        this = dict(m=SLOTS * m, sums=[])
        if more:
            arrays = later
        near = [swap_y(b, 0), swap_y(b, 1)]
        bz = cross_z(crossing)
        this["first"] = [b, *near, bz]
        ready = []
        if last is not None:
            ready = [*ready, step(1, last)[0]]
        near, bz = wait_for((near, bz), *ready)
        going, this["second"] = gather_second(near, bz, swap_y)
        if last is not None:
            last["third"] = wait_for(last["third"], *going)
            sums = step(2, last)
            swapped = flip_core(sums[1])
        if more:
            arrays = rows_second(wait_for(arrays, near[0]))
        ready = arrays[4:6] if more else []
        if last is not None:
            product, came = return_first(plan, sums, swapped)
        step(0, this)
        if last is not None:
            if back is not None:
                out.append(return_last(plan, *back))
            sent, came = return_second(plan, product, wait_for(came, this["sums"][0], *out))
            back = product, came
            ready = [*ready, sent]
        both = wait_for(this["second"], this["sums"][0], *ready)
        this["third"] = gather_third(both, SLOTS * m, swap_y)
        if more:
            arrays = rows_third(wait_for(arrays, this["sums"][0]))
        last = this
    sums, back = finish(last, back)
    product, came = return_first(plan, sums, flip_core(sums[1]))
    if back is not None:
        out.append(return_last(plan, *back))
    came = return_second(plan, product, wait_for(came, *out))[1]
    out.append(return_last(plan, product, return_third(plan, product, came)))
    out = [o.reshape(local_tiles, -1, cols) for o in out]
    return jnp.concatenate(out, axis=1).reshape(local_tiles * TILE, cols)


def solution(mesh):
    in_specs = (P("row", "col"), P(), P("row", None, "col"))
    out_specs = P("row", "col")
    return jax.shard_map(
        on_device, mesh=mesh, in_specs=in_specs, out_specs=out_specs, check_vma=False
    )
```

```python
import functools

import jax
import jax.numpy as jnp
import numpy as np
from jax import lax
from jax.experimental import pallas as pl
from jax.experimental.pallas import tpu as pltpu
from jax.sharding import PartitionSpec as P

TILE = 128
SLOTS = 4
CHUNKS = (80, 48)
BRIEF = pl.CostEstimate(flops=1, bytes_accessed=1, transcendentals=0)

PLACES = [
    (zl, x, zh, y, c)
    for zl in range(2)
    for x in range(4)
    for zh in range(2)
    for y in range(4)
    for c in range(2)
]


def send(a, to):
    index = {p: i for i, p in enumerate(PLACES)}
    return lax.ppermute(a, ("row", "col"), [(i, index[to(*p)]) for p, i in index.items()])


def other_of(i, ring):
    return (i + (1 if i % 2 == ring else 3)) % 4


def swap_x(a, ring):
    return send(a, lambda zl, x, zh, y, c: (zl, other_of(x, ring), zh, y, c))


def swap_y(a, ring):
    return send(a, lambda zl, x, zh, y, c: (zl, x, zh, other_of(y, ring), c))


def flip_z(a):
    return send(a, lambda zl, x, zh, y, c: (1 - zl, x, zh, y, c))


def cross_z(a):
    return send(a, lambda zl, x, zh, y, c: (1 - zl, x, 1 - zh, y, c))


def flip_core(a):
    return send(a, lambda zl, x, zh, y, c: (zl, x, zh, y, 1 - c))


def split(v):
    hi = v.astype(jnp.bfloat16)
    return hi, (v - hi.astype(jnp.float32)).astype(jnp.bfloat16)


def product_kernel(blocks, n_arrays, first, at_ref, *refs):
    arrays, (own_ref, far_ref), refs = refs[:n_arrays], refs[n_arrays : n_arrays + 2], refs[n_arrays + 2 :]
    adds, (out_own, out_far) = refs[:2], refs[-2:]
    step = pl.program_id(0)

    for i, block in enumerate(blocks):

        @pl.when(step == i)
        def _():
            parts = [arrays[array][lo : lo + size] for array, lo, size in block]
            a_hi, a_lo = split(parts[0] if len(parts) == 1 else jnp.concatenate(parts, axis=0))
            a_both = jnp.concatenate([a_hi, a_lo], axis=0)
            m = a_hi.shape[0]
            for j, (rhs, out) in enumerate(((own_ref, out_own), (far_ref, out_far))):
                b_hi, b_lo = split(rhs[...])
                dot = functools.partial(jnp.dot, preferred_element_type=jnp.float32)
                upper = dot(a_both, b_hi)
                term = upper[:m] + (upper[m:] + dot(a_hi, b_lo))
                if i == 0:
                    out[...] = term if first else adds[j][...] + term
                else:
                    out[...] += term


def products(arrays, blocks, at, own, far, sums):
    n = len(blocks)
    m = sum(size for _, _, size in blocks[0])
    width = arrays[0].shape[1]
    cols = own.shape[1]
    vmem = pl.BlockSpec(memory_space=pltpu.VMEM)
    return pl.pallas_call(
        functools.partial(product_kernel, blocks, len(arrays), not sums),
        grid_spec=pltpu.PrefetchScalarGridSpec(
            num_scalar_prefetch=1,
            grid=(n,),
            in_specs=[vmem] * len(arrays)
            + [pl.BlockSpec((width, cols), lambda s, at: (at[s], 0))] * 2
            + [vmem] * len(sums),
            out_specs=[vmem] * 2,
        ),
        out_shape=[jax.ShapeDtypeStruct((m, cols), jnp.float32)] * 2,
        compiler_params=pltpu.CompilerParams(vmem_limit_bytes=50 * 1024 * 1024),
        cost_estimate=BRIEF,
        name="products",
    )(at, *arrays, own, far, *sums)


def small_kernel(body, plan, shapes, operands, after=(), name=None):
    def kernel(plan_ref, *refs):
        body(plan_ref, refs[: len(operands)], refs[len(operands) + len(after) :])

    out = pl.pallas_call(
        kernel,
        in_specs=[pl.BlockSpec(memory_space=pltpu.SMEM)]
        + [pl.BlockSpec(memory_space=pltpu.VMEM)] * len(operands)
        + [pl.BlockSpec(memory_space=pl.ANY)] * len(after),
        out_specs=[pl.BlockSpec(memory_space=pltpu.VMEM)] * len(shapes),
        out_shape=[jax.ShapeDtypeStruct(s, jnp.float32) for s in shapes],
        compiler_params=pltpu.CompilerParams(vmem_limit_bytes=24 * 1024 * 1024),
        cost_estimate=pl.CostEstimate(
            flops=0, bytes_accessed=4 * sum(int(np.prod(s)) for s in shapes), transcendentals=0
        ),
        name=name,
    )(plan, *operands, *after)
    return out


def wait_for(value, *others):
    return lax.optimization_barrier((value, others))[0]


def gather_second(near, other, swap, pieces=1):
    going = [join(other, half(near[1 - i], i, pieces)) for i in range(2)]
    return going, [swap(a, i) for i, a in enumerate(going)]


def gather_third(both, rows, swap, pieces=1):
    return swap(half(both[1][:rows], 0, pieces), 0), swap(half(both[0][:rows], 1, pieces), 1)


def join(*arrays):
    return jnp.concatenate(arrays, axis=0)


def half(a, which, pieces):
    cut = a.reshape(pieces, 2, -1, a.shape[1])[:, which]
    return cut.reshape(-1, a.shape[1])


def pick(plan, m, arrays, after):
    width = arrays[0].shape[1]
    h = m // 2
    where = [
        [(0, 0, m)],
        [(1, 0, m)],
        [(2, 0, m)],
        [(4, 0, m)],
        [(4, 2 * m, h), (5, 2 * m, h)],
        [(6, 0, h), (7, 0, h)],
        [(3, 0, m)],
        [(5, 0, m)],
    ]

    def body(plan_ref, ins, outs):
        for s in range(2 * SLOTS):
            place = plan_ref[s]
            out, to = outs[s // SLOTS], s % SLOTS * m
            for i, parts in enumerate(where):

                @pl.when(place // 2 == i)
                def _():
                    at = to
                    for array, lo, size in parts:
                        rows = pl.ds(pl.multiple_of(lo + place % 2 * size, 8), size)
                        out[at : at + size] = ins[array][rows]
                        at += size

    return small_kernel(body, plan, [(SLOTS * m, width)] * 2, arrays, after, name="pick")


GROUPS = [[(0, 0), (0, 1), (0, 3), (1, 0)], [(1, 1), (1, 3), (0, 2)], [(1, 2)]]


def share(plan_ref, ring, dz, product, lo, hi, out, at, pitch, arrived=None):
    for j in range(2):
        slot = plan_ref[2 * SLOTS + ring * 4 + dz * 2 + j]
        rows = pl.ds(at + j * pitch, hi - lo)

        @pl.when(slot >= 0)
        def _():
            out[rows] = product[slot, lo:hi]

        @pl.when(slot < 0)
        def _():
            if arrived is None:
                out[rows] = jnp.zeros((hi - lo, product.shape[2]), jnp.float32)
            else:
                out[rows] = arrived(j)


def return_first(plan, sums, swapped):
    m, cols = sums[0].shape[0] // SLOTS, sums[0].shape[1]
    h = m // 2

    def body(plan_ref, ins, outs):
        mine, theirs = ins
        product, out_a, out_b = outs
        for s in range(SLOTS):
            rows = slice(s * m, (s + 1) * m)
            product[s] = mine[rows] + theirs[rows]
        share(plan_ref, 2, 1, product, 0, h, out_a, 0, h)
        share(plan_ref, 2, 1, product, h, m, out_b, 0, h)

    shapes = [(SLOTS, m, cols), (m, cols), (m, cols)]
    product, a, b = small_kernel(body, plan, shapes, [sums[0], swapped], name="return_first")
    return product, [swap_x(a, 0), swap_x(b, 1)]


def near_shares(plan_ref, dz, product, out_a, out_b, from_a, from_b):
    m = product.shape[1]
    h = m // 2
    share(plan_ref, 1, dz, product, 0, h, out_a, 0, m)
    share(plan_ref, 1, dz, product, h, m, out_a, h, m, from_b)
    share(plan_ref, 3, dz, product, 0, h, out_b, 0, m, from_a)
    share(plan_ref, 3, dz, product, h, m, out_b, h, m)


def return_second(plan, product, came):
    _, m, cols = product.shape
    h = m // 2

    def body(plan_ref, ins, outs):
        product, a, b = ins
        out_a, out_b = outs
        part = lambda ref: lambda j: ref[j * h : (j + 1) * h]
        near_shares(plan_ref, 1, product, out_a, out_b, part(a), part(b))
        share(plan_ref, 2, 0, product, 0, h, out_a, 2 * m, h)
        share(plan_ref, 2, 0, product, h, m, out_b, 2 * m, h)

    a, b = small_kernel(
        body, plan, [(3 * m, cols)] * 2, [product, *came], name="return_second"
    )
    return a, [swap_x(a, 0), swap_x(b, 1)]


def return_third(plan, product, came):
    _, m, cols = product.shape
    h = m // 2

    def body(plan_ref, ins, outs):
        product, a, b = ins
        out_a, out_b, across = outs
        part = lambda ref: lambda j: ref[2 * m + j * h : 2 * m + (j + 1) * h]
        near_shares(plan_ref, 0, product, out_a, out_b, part(a), part(b))
        both = lambda j: a[j * m : (j + 1) * m] + b[j * m : (j + 1) * m]
        share(plan_ref, 0, 1, product, 0, m, across, 0, m, both)

    a, b, across = small_kernel(
        body, plan, [(2 * m, cols)] * 3, [product, *came], name="return_third"
    )
    return [swap_x(a, 0), swap_x(b, 1), flip_z(across)]


def return_last(plan, product, came):
    _, m, cols = product.shape

    def body(plan_ref, ins, outs):
        product, *came = ins
        (total,) = outs
        rows = lambda j: slice(j * m, (j + 1) * m)
        arrived = lambda j: came[0][rows(j)] + came[1][rows(j)] + came[2][rows(j)]
        share(plan_ref, 0, 0, product, 0, m, total, 0, m, arrived)

    (total,) = small_kernel(body, plan, [(2 * m, cols)], [product, *came], name="return_last")
    return total


def on_device(amplitudes, labels, integrals):
    flat = labels[:, 0]
    n_tiles = flat.shape[0]
    local_tiles = amplitudes.shape[0] // TILE
    width = amplitudes.shape[1]
    cols = integrals.shape[2]
    row = lax.axis_index("row")
    col = lax.axis_index("col")
    zl, x = row // 4, row % 4
    zh, y, core = col // 8, col // 2 % 4, col % 2

    ids = np.arange(n_tiles, dtype=np.int32)
    same = (flat[:, None] == flat[None, :]) & (ids[None, :] < ids[:, None])
    rank = jnp.sum(same.astype(jnp.int32), axis=1)
    ring = (ids // 2 % 4 - x) * (1 - 2 * (x % 2)) % 4
    place = ring * 4 + ((ids // 8) ^ zl) * 2 + ids % 2
    slot = np.arange(2 * SLOTS, dtype=np.int32)
    target = jnp.where(slot < SLOTS, row, (1 - zl) * 4 + x)
    hit = (flat[None, :] == target[:, None]) & (rank[None, :] == (slot % SLOTS)[:, None])
    wanted = jnp.sum(jnp.where(hit, place[None, :], 0), axis=1)
    held = jnp.where(flat == row, rank, -1)
    slots = jnp.sum(jnp.where(place[None, :] == ids[:, None], held[None, :], 0), axis=1)
    plan = jnp.concatenate([wanted, slots])

    tiles = amplitudes.reshape(local_tiles, TILE, width)
    starts = [sum(CHUNKS[:i]) for i in range(len(CHUNKS))]
    pieces = [tiles[:, s : s + m].reshape(-1, width) for s, m in zip(starts, CHUNKS)]

    own = integrals.reshape(16 * width, cols)
    far = flip_core(own)
    at = []
    for group in GROUPS:
        gz, ring = np.array(group, np.int32).T
        places = (zh ^ gz) * 4 + (y + ring * (1 - 2 * (y % 2))) % 4
        at.append(places * 2 + core)

    def rows_first(piece, before=None):
        beside, later = (), ()
        if before is not None:
            beside, later = before[1:4], before[4:6]
        other = flip_z(wait_for(piece, *beside))
        own = wait_for(piece, *later)
        return [piece, other, swap_x(own, 0), swap_x(own, 1)]

    def rows_second(arrays):
        return arrays + gather_second(arrays[2:4], arrays[1], swap_x, local_tiles)[1]

    def rows_third(arrays):
        rows = arrays[1].shape[0]
        return arrays + list(gather_third(arrays[4:6], rows, swap_x, local_tiles))

    def step(group, last):
        m, h = last["m"], last["m"] // 2
        if group == 0:
            arrays, blocks = last["first"], [[(i, 0, m)] for i in range(4)]
        elif group == 1:
            arrays, blocks = last["second"], [[(0, 0, m)], [(1, 0, m)], [(0, m, h), (1, m, h)]]
        else:
            arrays, blocks = last["third"], [[(0, 0, h), (1, 0, h)]]
        last["sums"] = products(arrays, blocks, at[group], own, far, last["sums"])
        return last["sums"]

    def finish(last, back):
        sums = step(1, last)
        if back is not None:
            product, came = back
            back = product, return_third(plan, product, wait_for(came, sums[0]))
        return step(2, last), back

    arrays = rows_third(rows_second(rows_first(pieces[0])))
    out, last, back = [], None, None
    for k, m in enumerate(CHUNKS):
        more = k + 1 < len(CHUNKS)
        after = () if last is None else (last["second"][0], last["sums"][0])
        if more:
            later = rows_first(pieces[k + 1], arrays)
            after = (*after, later[1])
        b, crossing = pick(plan, m, arrays, after)
        this = dict(m=SLOTS * m, sums=[])
        if more:
            arrays = later
        near = [swap_y(b, 0), swap_y(b, 1)]
        bz = cross_z(crossing)
        this["first"] = [b, *near, bz]
        ready = []
        if last is not None:
            ready = [*ready, step(1, last)[0]]
        near, bz = wait_for((near, bz), *ready)
        going, this["second"] = gather_second(near, bz, swap_y)
        if last is not None:
            last["third"] = wait_for(last["third"], *going)
            sums = step(2, last)
            swapped = flip_core(sums[1])
        if more:
            arrays = rows_second(wait_for(arrays, near[0]))
        ready = arrays[4:6] if more else []
        if last is not None:
            product, came = return_first(plan, sums, swapped)
        step(0, this)
        if last is not None:
            if back is not None:
                out.append(return_last(plan, *back))
            sent, came = return_second(plan, product, wait_for(came, this["sums"][0], *out))
            back = product, came
            ready = [*ready, sent]
        both = wait_for(this["second"], this["sums"][0], *ready)
        this["third"] = gather_third(both, SLOTS * m, swap_y)
        if more:
            arrays = rows_third(wait_for(arrays, this["sums"][0]))
        last = this
    sums, back = finish(last, back)
    product, came = return_first(plan, sums, flip_core(sums[1]))
    if back is not None:
        out.append(return_last(plan, *back))
    came = return_second(plan, product, wait_for(came, *out))[1]
    out.append(return_last(plan, product, return_third(plan, product, came)))
    out = [o.reshape(local_tiles, -1, cols) for o in out]
    return jnp.concatenate(out, axis=1).reshape(local_tiles * TILE, cols)


def solution(mesh):
    in_specs = (P("row", "col"), P(), P("row", None, "col"))
    out_specs = P("row", "col")
    return jax.shard_map(
        on_device, mesh=mesh, in_specs=in_specs, out_specs=out_specs, check_vma=False
    )
```
